128 devices in a mesh: lat: 16 (over y, x_hi, core), lon: 8 (over z, x_lo).
Axes of the slice: x: 4 (x_hi: 2, x_lo: 2; x = x_hi * 2 + x_lo), y: 4, z: 4, core: 2. Of those that a mesh axis runs over, the one named last changes fastest.
Arguments:
- state: float32 [3, 1440, 256, 128], P(None, 'lon', 'lat'), may hold values from -6 to 6
- cutoffs: int32 [256], P('lat'), may hold values from 32 to 180, as said below
Outputs:
- updated: float32 [3, 1440, 256, 128], P(None, 'lon', 'lat')
The draws below stay inside these ranges and needn't reach their ends.
Inputs may be any that keep to these rules, and one draw needn't show every extreme that they name: `cutoffs`: only rows poleward of 45 degrees read their cutoff.
All inputs are finite; a program needn't handle non-finite values.
Results may differ from the reference program's by a relative error of at most 0.00011.
Values sent between devices are 32-bit elements; how exact they have to be, the bound alone decides.
No kernel may reach another device: no remote copies, remote signals or barrier semaphores. Data moves between devices by JAX's collectives and lax.ppermute only.
A program may use at most 128 MiB of HBM per device.

```python
import jax
import jax.numpy as jnp
from jax import lax

NLON = 1440
LEV = 128
SUBSTEPS = 2
NLAT = 256


def shared_cutoffs(key):
    lowest = max(1, NLON // 45)
    highest = NLON // 8
    table = jax.random.randint(jax.random.fold_in(key, 11), (NLAT,), lowest, highest + 1, dtype=jnp.int32)
    rows = jnp.arange(NLAT, dtype=jnp.int32)
    table = jnp.where(rows == 0, highest, table)
    table = jnp.where(rows == NLAT - 1, lowest, table)
    return table


def band_wave(key, cutoff_table, offset_low, offset_high):
    offsets = jax.random.randint(key, (3, 1, NLAT, LEV), offset_low, offset_high + 1, dtype=jnp.int32)
    return jnp.clip(cutoff_table[None, None, :, None] + offsets, 1, NLON // 2)


def one_mode(key, wavenumber, amplitude):
    phase = jax.random.uniform(key, (3, 1, NLAT, LEV), jnp.float32, -jnp.pi, jnp.pi)
    column = jnp.arange(NLON, dtype=jnp.int32)[None, :, None, None]
    turns = wavenumber * column % NLON
    angle = turns.astype(jnp.float32) * (2.0 * jnp.pi / NLON) + phase
    return amplitude * jnp.cos(angle)


def draw_cutoffs(key, part):
    return shared_cutoffs(key)


def draw_state(key, part):
    cutoff_table = shared_cutoffs(key)
    key = jax.random.fold_in(key, 7)
    streams = jax.random.split(key, 10)
    small_shape = (3, 1, NLAT, LEV)
    full_shape = (3, NLON, NLAT, LEV)
    near_wave = band_wave(streams[0], cutoff_table, -1, 2)
    next_wave = band_wave(streams[1], cutoff_table, -1, 2)
    high_wave = jax.random.randint(streams[2], small_shape, NLON // 4, NLON // 2 + 1, dtype=jnp.int32)
    noise = jnp.clip(0.8 * jax.random.normal(streams[3], full_shape, jnp.float32), -3.2, 3.2)
    near_amp = jax.random.uniform(streams[4], small_shape, jnp.float32, 0.6, 0.9)
    next_amp = jax.random.uniform(streams[5], small_shape, jnp.float32, 0.3, 0.6)
    high_amp = jax.random.uniform(streams[6], small_shape, jnp.float32, 0.4, 0.8)
    total = noise + one_mode(streams[7], near_wave, near_amp)
    total = total + one_mode(streams[8], next_wave, next_amp)
    total = total + one_mode(streams[9], high_wave, high_amp)
    return total.astype(jnp.float32)


def setup_inputs(seed: int = 0) -> dict:
    seeds = jax.random.split(jax.random.key(seed), 3)
    return {
        "state": draw_state(jax.random.fold_in(seeds[2], 71), 0),
        "cutoffs": draw_cutoffs(jax.random.fold_in(seeds[2], 71), 0),
    }


adv_coeff = 0.5
sound_coeff = 0.8
metric_cap = 2.0


def east_diff(field):
    return (jnp.roll(field, -1, axis=-2) - jnp.roll(field, 1, axis=-2)) * 0.5


def north_diff(field):
    widths = [(0, 0)] * (field.ndim - 1) + [(1, 1)]
    padded = jnp.pad(field, widths)
    return (padded[..., 2:] - padded[..., :-2]) * 0.5


def reference(state, cutoffs):
    row_index = jnp.arange(NLAT, dtype=jnp.int32)
    latitude = (-90.0 + (row_index.astype(jnp.float32) + 0.5) * (180.0 / NLAT)) * (jnp.pi / 180.0)
    metric = 1.0 / jnp.maximum(jnp.cos(latitude), 1.0 / metric_cap)
    polar = (row_index < NLAT // 4) | (row_index >= NLAT - NLAT // 4)
    wave = jnp.arange(NLON // 2 + 1, dtype=jnp.int32).astype(jnp.float32)
    limit = cutoffs.astype(jnp.float32)[None, :]
    factor = jnp.where(wave[:, None] <= limit, 1.0, (limit / jnp.maximum(wave, 1.0)[:, None]) ** 2)

    def one_level(fields):
        wind_u = fields[0]
        wind_v = fields[1]
        advected = fields - adv_coeff * (metric * wind_u * east_diff(fields) + wind_v * north_diff(fields))
        wind_u = advected[0]
        wind_v = advected[1]
        theta = advected[2]
        for substep in range(SUBSTEPS):
            wind_u = wind_u - sound_coeff * metric * east_diff(theta)
            wind_v = wind_v - sound_coeff * north_diff(theta)
            theta = theta - sound_coeff * (metric * east_diff(wind_u) + north_diff(wind_v))
        acoustic = jnp.stack([wind_u, wind_v, theta])
        spectrum = jnp.fft.rfft(acoustic, axis=-2)
        filtered = jnp.fft.irfft(spectrum * factor[None], n=NLON, axis=-2).astype(acoustic.dtype)
        return jnp.where(polar[None, None, :], filtered, acoustic)

    levels = jnp.moveaxis(state, 3, 0)
    finished = lax.map(one_level, levels)
    return jnp.moveaxis(finished, 0, 3)
```

```python
import functools

import jax
import jax.numpy as jnp
import numpy as np
from jax import lax
from jax.experimental import pallas as pl
from jax.experimental.pallas import tpu as pltpu
from jax.sharding import PartitionSpec as P

SUBSTEPS = 2
HALO = 1 + 2 * SUBSTEPS
ADV = 0.5
SOUND = 0.8
CAP = 2.0
LEAD = 16
GROUP = 8
MIB = 1024 * 1024

f32 = jnp.float32
bf16 = jnp.bfloat16


def params(mib):
    return pltpu.CompilerParams(vmem_limit_bytes=mib * MIB)


def vmem():
    return pl.BlockSpec(memory_space=pltpu.VMEM)


def smem():
    return pl.BlockSpec(memory_space=pltpu.SMEM)


def edge_row(d):
    return jnp.where(d < 4, d, d + 8)


def inner_row(d):
    return d + 4


EDGE = [d if d < 4 else d + 8 for d in range(GROUP)]
INNER = [d + 4 for d in range(GROUP)]


def padded(cols):
    return -(-cols // 8) * 8


def window(cols):
    return -(-(8 + cols + HALO) // 8) * 8


def cost(micros):
    return pl.CostEstimate(flops=0, bytes_accessed=int(micros * 3.69e6), transcendentals=0)


def any_space():
    return pl.BlockSpec(memory_space=pltpu.MemorySpace.HBM)


def send_kernel(cols, rows, x_ref, west_ref, east_ref, _, north_ref, south_ref, hold, sem):
    loads = [pltpu.make_async_copy(x_ref.at[c], hold.at[c], sem.at[c]) for c in range(3)]
    for copy in loads:
        copy.start()

    def put(ref, at, c, r):
        ref[at, pl.ds(8, cols)] = hold[c, pl.ds(r, cols, stride=rows), :]
        ref[at, pl.ds(8 - HALO, HALO)] = west_ref[c, pl.ds(r, HALO, stride=rows), :]
        ref[at, pl.ds(8 + cols, HALO)] = east_ref[c, pl.ds(r, HALO, stride=rows), :]

    top = rows - HALO + 1
    for c in range(3):
        loads[c].wait()
        for k in range(HALO - 1):
            put(north_ref, (HALO - 1) * c + k, c, k)
            put(south_ref, (HALO - 1) * c + k, c, top + k)
    put(north_ref, 3 * (HALO - 1), 2, HALO - 1)
    put(south_ref, 3 * (HALO - 1), 2, rows - HALO)


def row_sends(flat, west, east_, after, cols, rows):
    lev = flat.shape[-1]
    edge = jax.ShapeDtypeStruct((3 * (HALO - 1) + 1, window(cols), lev), f32)
    return pl.pallas_call(
        functools.partial(send_kernel, cols, rows),
        in_specs=[any_space(), vmem(), vmem(), any_space()],
        out_specs=[vmem()] * 2,
        out_shape=[edge, edge],
        scratch_shapes=[pltpu.VMEM(flat.shape, f32), pltpu.SemaphoreType.DMA((3,))],
        compiler_params=params(60),
        cost_estimate=cost(4),
    )(flat, west, east_, after)


def east(W, r):
    cols = W.shape[1] - 16
    return W[r, pl.ds(9, cols)] - W[r, pl.ds(7, cols)]


def stage_steps(metric_ref, base, U, V, T, A, B, C, keep):
    mid = pl.ds(8, U.shape[1] - 16)

    def metric(i):
        return metric_ref[i + (HALO - base)]

    def advect(i, fields=None):
        mu = metric(i) * (0.5 * ADV) * U[i, mid]
        nv = (0.5 * ADV) * V[i, mid]
        for W, out in fields or ((U, A), (V, B), (T, C)):
            out[i, mid] = W[i, mid] - (mu * east(W, i) + nv * (W[i + 1, mid] - W[i - 1, mid]))

    def advect_theta(i):
        advect(i, ((T, C),))

    def wind_u(i):
        A[i, mid] = A[i, mid] - (metric(i) * (0.5 * SOUND)) * east(C, i)

    def wind_v(i):
        B[i, mid] = keep(i, B[i, mid] - (0.5 * SOUND) * (C[i + 1, mid] - C[i - 1, mid]))

    def theta(i):
        m = metric(i) * (0.5 * SOUND)
        C[i, mid] = keep(i, C[i, mid] - (m * east(A, i) + (0.5 * SOUND) * (B[i + 1, mid] - B[i - 1, mid])))

    return advect, advect_theta, wind_u, wind_v, theta


def sweep(fn, *spans):
    for lo, hi in spans:

        def step(i, carry):
            fn(i)
            return carry

        lax.fori_loop(lo, hi, step, 0)


def inner_kernel(
    cols, rows, metric_ref, x_ref, west_ref, east_ref, _, u_ref, v_ref, theta_ref, rim_ref, raw_ref, *scratch
):
    U, V, T, A, B, C, hold, sem, out_sem = scratch
    own = slice(LEAD, LEAD + cols)
    wide = pl.ds(LEAD - 8, window(cols))
    loads = [pltpu.make_async_copy(x_ref.at[c], hold.at[c], sem.at[c]) for c in range(3)]
    for copy in loads:
        copy.start()
    outs = []
    for c, W in enumerate((U, V, T)):
        loads[c].wait()

        def fill(r, carry, c=c, W=W):
            W[r, own] = hold[c, pl.ds(r, cols, stride=rows), :]
            W[r, pl.ds(LEAD - HALO, HALO)] = west_ref[c, pl.ds(r, HALO, stride=rows), :]
            W[r, pl.ds(LEAD + cols, HALO)] = east_ref[c, pl.ds(r, HALO, stride=rows), :]
            return carry

        lax.fori_loop(0, rows, fill, 0)
        for k, at in ((0, 0), (1, rows - 2)):
            outs.append((W.at[pl.ds(at, 2), wide], raw_ref.at[c, pl.ds(2 * k, 2)]))
    advect, _, wind_u, wind_v, theta = stage_steps(metric_ref, 0, U, V, T, A, B, C, lambda r, x: x)
    sweep(advect, (1, rows - 1))
    sweep(wind_u, (1, rows - 1))
    sweep(wind_v, (2, rows - 2))
    sweep(theta, (3, rows - 3))
    sweep(wind_u, (3, rows - 3))
    sweep(wind_v, (4, rows - 4))
    sweep(theta, (5, rows - 5))
    for c, W in enumerate((A, B, C)):
        for k, at in ((0, 1), (1, rows - 6)):
            outs.append((W.at[pl.ds(at, 5), wide], rim_ref.at[c, pl.ds(5 * k, 5)]))
    outs = [pltpu.make_async_copy(a, b, out_sem.at[i]) for i, (a, b) in enumerate(outs)]
    for copy in outs:
        copy.start()
    pad = padded(cols)
    for d in range(GROUP):
        u_ref[d, pl.ds(0, cols)] = A[INNER[d], own]
        v_ref[d, pl.ds(0, cols)] = B[INNER[d], own]
        theta_ref[d, pl.ds(0, cols)] = C[INNER[d], own]
    for copy in outs:
        copy.wait()


def inner_rows(metric, flat, west, east_, after, cols, rows):
    lev = flat.shape[-1]
    pad = padded(cols)
    wide = window(cols)
    shapes = [(GROUP, pad, lev)] * 3 + [(3, 10, wide, lev), (3, 4, wide, lev)]
    return pl.pallas_call(
        functools.partial(inner_kernel, cols, rows),
        in_specs=[smem(), any_space(), vmem(), vmem(), any_space()],
        out_specs=[vmem()] * 3 + [any_space()] * 2,
        out_shape=[jax.ShapeDtypeStruct(s, f32) for s in shapes],
        scratch_shapes=[pltpu.VMEM((rows, LEAD + wide, lev), f32)] * 6
        + [pltpu.VMEM(flat.shape, f32), pltpu.SemaphoreType.DMA((3,)), pltpu.SemaphoreType.DMA((12,))],
        compiler_params=params(60),
        cost_estimate=cost(9),
    )(metric, flat, west, east_, after)


def edge_kernel(
    cols, rows, ids_ref, metric_ref, raw_ref, rim_ref, hn_ref, hs_ref, u_ref, v_ref, theta_ref, _, send_ref, out_ref, *scratch
):
    U, V, T, A, B, C, hold, moved, sem, move_sem, out_sem = scratch
    own = slice(LEAD, LEAD + cols)
    wide = pl.ds(LEAD - 8, window(cols))
    pad = padded(cols)
    count = HALO - 1
    loads = []
    for c, W in enumerate((U, V, T)):
        loads.append((hn_ref.at[pl.ds(count * c, count)], W.at[pl.ds(1, count), wide]))
        loads.append((hs_ref.at[pl.ds(count * c, count)], W.at[pl.ds(HALO + rows, count), wide]))
        loads.append((raw_ref.at[c, pl.ds(0, 2)], W.at[pl.ds(HALO, 2), wide]))
        loads.append((raw_ref.at[c, pl.ds(2, 2)], W.at[pl.ds(HALO + rows - 2, 2), wide]))
    loads.append((hn_ref.at[pl.ds(3 * count, 1)], T.at[pl.ds(0, 1), wide]))
    loads.append((hs_ref.at[pl.ds(3 * count, 1)], T.at[pl.ds(2 * HALO + rows - 1, 1), wide]))
    for c, W in enumerate((A, B, C)):
        loads.append((rim_ref.at[c, pl.ds(0, 5)], W.at[pl.ds(HALO + 1, 5), wide]))
        loads.append((rim_ref.at[c, pl.ds(5, 5)], W.at[pl.ds(HALO + rows - 6, 5), wide]))
    loads = [pltpu.make_async_copy(a, b, sem.at[i]) for i, (a, b) in enumerate(loads)]
    for copy in loads:
        copy.start()
    for copy in loads:
        copy.wait()
    has_north = jnp.where(ids_ref[1] > 0, 1.0, 0.0)
    has_south = jnp.where(ids_ref[2] > 0, 1.0, 0.0)

    def keep(i, x):
        return x * jnp.where(i >= HALO + rows, has_south, jnp.where(i < HALO, has_north, 1.0))

    advect, advect_theta, wind_u, wind_v, theta = stage_steps(metric_ref, HALO, U, V, T, A, B, C, keep)

    def ends(fn, lo, hi):
        sweep(fn, (HALO + lo, HALO + hi), (HALO + rows - hi, HALO + rows - lo))

    ends(advect, -3, 1)
    ends(advect_theta, -4, -3)
    ends(wind_u, -2, 1)
    ends(wind_v, -3, 2)
    ends(theta, -2, 3)
    ends(wind_u, 0, 3)
    ends(wind_v, -1, 4)
    ends(theta, 0, 5)

    @pl.when(ids_ref[3] != 0)
    def _():
        inside = pltpu.make_async_copy(
            theta_ref.at[pl.ds(1, GROUP - 2)], send_ref.at[pl.ds(1, GROUP - 2), pl.ds(3 * pad, pad)], move_sem.at[0]
        )
        inside.start()
        for d in range(GROUP):
            for c, W in enumerate((A, B, C)):
                send_ref[d, pl.ds(c * pad, cols)] = W[EDGE[d] + HALO, own]
        for d in (0, GROUP - 1):
            send_ref[d, pl.ds(3 * pad, cols)] = C[INNER[d] + HALO, own]
        inside.wait()

    @pl.when(ids_ref[3] == 0)
    def _():
        inside = [
            pltpu.make_async_copy(ref, moved.at[:, pl.ds(c * pad, pad)], move_sem.at[c])
            for c, ref in enumerate((u_ref, v_ref, theta_ref))
        ]
        for copy in inside:
            copy.start()
        for copy in inside:
            copy.wait()
        outs = [pltpu.make_async_copy(hold.at[c], out_ref.at[c], out_sem.at[c]) for c in range(3)]
        for c, W in enumerate((A, B, C)):
            for d in range(GROUP):
                hold[c, pl.ds(EDGE[d], cols, stride=rows), :] = W[EDGE[d] + HALO, own]
                if c == 2 and d in (0, GROUP - 1):
                    value = C[INNER[d] + HALO, own]
                else:
                    value = moved[d, pl.ds(c * pad, cols)]
                hold[c, pl.ds(INNER[d], cols, stride=rows), :] = value
            outs[c].start()
        for out in outs:
            out.wait()


def edge_rows(ids, metric, raw, rim, hn, hs, inner, after, cols, rows):
    lev = raw.shape[-1]
    pad = padded(cols)
    whole = (3, cols * rows, lev)
    return pl.pallas_call(
        functools.partial(edge_kernel, cols, rows),
        in_specs=[smem(), smem()] + [any_space()] * 8,
        out_specs=[vmem(), any_space()],
        out_shape=[jax.ShapeDtypeStruct((GROUP, 4 * pad, lev), f32), jax.ShapeDtypeStruct(whole, f32)],
        scratch_shapes=[pltpu.VMEM((rows + 2 * HALO, LEAD + window(cols), lev), f32)] * 6
        + [pltpu.VMEM(whole, f32), pltpu.VMEM((GROUP, 3 * pad, lev), f32)]
        + [pltpu.SemaphoreType.DMA((n,)) for n in (20, 3, 3)],
        compiler_params=params(60),
        cost_estimate=cost(8),
    )(ids, metric, raw, rim, hn, hs, *inner, after)


def offset_tables(length):
    half = length // 2
    pad = -(-half // 256) * 256
    n = np.arange(2 * pad) - pad
    tables = []
    for first in (0, 1):
        wave = np.arange(first, half + 1, 2)
        weight = np.where((wave == 0) | (wave == half), 1.0, 2.0) / length
        angle = (wave[:, None] * n[None, :]) % length * (2.0 * np.pi / length)
        tables.append((wave, (np.cos(angle) * weight[:, None]).astype(np.float32)))
    return tables


def offset_values(limits, length):
    values = []
    for wave, table in offset_tables(length):
        w = jnp.asarray(wave, f32)
        lim = limits[:, None]
        factor = jnp.where(w[None, :] <= lim, 1.0, (lim / jnp.maximum(w, 1.0)[None, :]) ** 2)
        values.append(jnp.dot(factor, jnp.asarray(table), precision=lax.Precision.HIGHEST, preferred_element_type=f32))
    return jnp.stack(values, axis=1)[:, :, None, :]


def skew(p, store):
    width = p.shape[-1]
    line = lax.broadcasted_iota(jnp.int32, (8, width), 0)
    x = jnp.broadcast_to(p, (8, width))
    for bit in range(3):
        x = jnp.where((line & (1 << bit)) != 0, pltpu.roll(x, 1 << bit, 1), x)
    for pair in range(8):
        two = [pltpu.roll(x, 8 * g, 1)[:, 128:] if g else x[:, 128:] for g in (2 * pair, 2 * pair + 1)]
        y = jnp.concatenate(two, axis=0)
        hi = y.astype(bf16)
        store(16 * pair, hi, (y - hi.astype(f32)).astype(bf16))


def skew_kernel(p_ref, hi_ref, lo_ref):
    rows, parts, _, width = p_ref.shape
    for r in range(rows):
        for e in range(parts):

            def store(at, hi, lo, r=r, e=e):
                hi_ref[r, e, at : at + 16] = hi
                lo_ref[r, e, at : at + 16] = lo

            skew(p_ref[r, e], store)


def skewed(values):
    rows, parts, _, width = values.shape
    out = jax.ShapeDtypeStruct((rows, parts, 128, width - 128), bf16)
    return pl.pallas_call(
        skew_kernel,
        in_specs=[vmem()],
        out_specs=[vmem()] * 2,
        out_shape=[out, out],
        compiler_params=params(16),
    )(values)


def filter_kernel(groups, cols, hi_ref, lo_ref, x_ref, y_ref, S, D, Y, Z):
    quarter = GROUP // 2
    size = S.shape[0]
    lev = x_ref.shape[-1]
    pad = padded(cols)
    units = [u for _, members in groups for u in members]
    S[quarter * cols :] = jnp.zeros((size - quarter * cols, S.shape[1]), f32)
    D[quarter * cols :] = jnp.zeros((size - quarter * cols, S.shape[1]), f32)
    for b in range(quarter):
        at = slice(b * cols, (b + 1) * cols)
        for i, u in enumerate(units):
            lanes = slice(i * lev, (i + 1) * lev)
            one = x_ref[b, pl.ds(u * pad, cols)]
            two = x_ref[b + quarter, pl.ds(u * pad, cols)]
            S[at, lanes] = one + two
            D[at, lanes] = one - two
    tall = size // 128
    first = 0
    for row, members in groups:
        lanes = slice(first * lev, (first + len(members)) * lev)
        first += len(members)

        def matrix(ref, e, row=row):
            starts = [(tall - 1 - b) * 128 for b in range(tall)]
            return jnp.concatenate([ref[row, e, :, st : st + size] for st in starts], axis=0)

        for e, (src, dst) in enumerate(((S, Y), (D, Z))):
            x = src[:, lanes]
            xh = x.astype(bf16)
            xl = (x - xh.astype(f32)).astype(bf16)
            mh = matrix(hi_ref, e)
            left = jnp.concatenate([mh, mh, matrix(lo_ref, e)], axis=1)
            right = jnp.concatenate([xh, xl, xh], axis=0)
            dst[:, lanes] = jnp.dot(left, right, preferred_element_type=f32)
    for b in range(quarter):
        at = slice(b * cols, (b + 1) * cols)
        for i, u in enumerate(units):
            lanes = slice(i * lev, (i + 1) * lev)
            y = Y[at, lanes]
            z = Z[at, lanes]
            y_ref[b, pl.ds(u * pad, cols)] = y + z
            y_ref[b + quarter, pl.ds(u * pad, cols)] = y - z


def filtered(groups, hi, lo, whole, cols):
    _, tall, lev = whole.shape
    count = sum(len(members) for _, members in groups)
    work = pltpu.VMEM((hi.shape[-1] - 128 * 5, count * lev), f32)
    return pl.pallas_call(
        functools.partial(filter_kernel, groups, cols),
        in_specs=[vmem()] * 3,
        out_specs=vmem(),
        out_shape=jax.ShapeDtypeStruct(whole.shape, f32),
        scratch_shapes=[work] * 4,
        compiler_params=params(32),
    )(hi, lo, whole)


def join_kernel(cols, rows, ids_ref, y_ref, m_ref, _, out_ref, held, moved, result, sem, out_sem):
    @pl.when(ids_ref[3] != 0)
    def _():
        pad = padded(cols)
        copies = [pltpu.make_async_copy(y_ref.at[:, pl.ds(u * pad, pad)], held.at[u], sem.at[u]) for u in range(4)]
        copies += [pltpu.make_async_copy(m_ref.at[:, pl.ds(u * pad, pad)], moved.at[u], sem.at[4 + u]) for u in range(2)]
        outs = [pltpu.make_async_copy(result.at[c], out_ref.at[c], out_sem.at[c]) for c in range(3)]
        for copy in copies:
            copy.start()
        for c, inner, wait in ((0, moved.at[0], 4), (1, moved.at[1], 5), (2, held.at[3], 3)):
            copies[c].wait()
            copies[wait].wait()
            for d in range(GROUP):
                result[c, pl.ds(EDGE[d], cols, stride=rows), :] = held[c, d, 0:cols]
                result[c, pl.ds(INNER[d], cols, stride=rows), :] = inner[d, 0:cols]
            outs[c].start()
        for c in range(3):
            outs[c].wait()


def joined(ids, whole, moved, other, cols, rows):
    lev = whole.shape[-1]
    pad = padded(cols)
    return pl.pallas_call(
        functools.partial(join_kernel, cols, rows),
        in_specs=[smem()] + [any_space()] * 3,
        out_specs=any_space(),
        out_shape=jax.ShapeDtypeStruct(other.shape, f32),
        scratch_shapes=[
            pltpu.VMEM((4, GROUP, pad, lev), f32),
            pltpu.VMEM((2, GROUP, pad, lev), f32),
            pltpu.VMEM(other.shape, f32),
            pltpu.SemaphoreType.DMA((6,)),
            pltpu.SemaphoreType.DMA((3,)),
        ],
        input_output_aliases={3: 0},
        compiler_params=params(16),
    )(ids, whole, moved, other)


def tie_kernel(x_ref, _, out_ref):
    pass


def tied(x, y):
    return pl.pallas_call(
        tie_kernel,
        in_specs=[any_space()] * 2,
        out_specs=any_space(),
        out_shape=jax.ShapeDtypeStruct(x.shape, x.dtype),
        input_output_aliases={0: 0},
        compiler_params=params(1),
    )(x, y)


def swapped(x):
    return lax.all_to_all(x, "lon", split_axis=0, concat_axis=0, tiled=True)


def body(state, cutoffs):
    lat_count = lax.axis_size("lat")
    lon_count = lax.axis_size("lon")
    _, cols, rows, lev = state.shape
    total_lat = rows * lat_count
    total_lon = cols * lon_count
    band = lax.axis_index("lat")
    me = lax.axis_index("lon")
    quarter = lat_count // 4
    polar = (band < quarter) | (band >= lat_count - quarter)
    ids = jnp.stack([me, band, lat_count - 1 - band, polar.astype(jnp.int32)]).astype(jnp.int32)

    up = [(i, i + 1) for i in range(lat_count - 1)]
    down = [(j, i) for i, j in up]
    right = [(i, (i + 1) % lon_count) for i in range(lon_count)]
    left = [(j, i) for i, j in right]

    flat = state.reshape(3, cols * rows, lev)
    west = lax.ppermute(state[:, cols - HALO :].reshape(3, HALO * rows, lev), "lon", right)
    east_ = lax.ppermute(state[:, :HALO].reshape(3, HALO * rows, lev), "lon", left)
    outward = [(b, b + quarter) for b in range(quarter)]
    outward += [(b, b - quarter) for b in range(lat_count - quarter, lat_count)]
    inward = [(j, i) for i, j in outward]
    near = band * rows - HALO + jnp.arange(rows + 2 * HALO, dtype=jnp.int32)
    latitude = (-90.0 + (near.astype(f32) + 0.5) * (180.0 / total_lat)) * (jnp.pi / 180.0)
    metric = 1.0 / jnp.maximum(jnp.cos(latitude), 1.0 / CAP)

    wanted = jnp.stack([edge_row(me), inner_row(me)])
    chosen = wanted[:, None] == jnp.arange(rows, dtype=jnp.int32)[None, :]
    picked = jnp.sum(jnp.where(chosen, cutoffs.astype(f32)[None, :], 0.0), axis=1)
    offsets = offset_values(picked, total_lon)
    hi, lo = skewed(offsets)
    send_north, send_south = row_sends(flat, west, east_, lo, cols, rows)
    halo_north = lax.ppermute(send_south, "lat", up)
    halo_south = lax.ppermute(send_north, "lat", down)

    u, v, theta, rim, raw = inner_rows(metric, flat, west, east_, send_north, cols, rows)
    moved_u = lax.ppermute(u, "lat", outward)
    moved_v = lax.ppermute(v, "lat", outward)
    moved_offsets = lax.ppermute(offsets[1:], "lat", outward)
    pieces, other = edge_rows(ids, metric, raw, rim, halo_north, halo_south, (u, v, theta), lo, cols, rows)

    def near_pole(pieces):
        return filtered(((0, (0, 1, 2)), (1, (3,))), hi, lo, swapped(pieces), cols)

    def elsewhere(u, v, offsets):
        moved = jnp.concatenate([u, v], axis=1)
        return swapped(filtered(((0, (0, 1)),), *skewed(offsets), swapped(moved), cols))

    pieces = lax.cond(polar, near_pole, lambda pieces: pieces, pieces)
    moved_u = tied(moved_u, pieces)
    moved = lax.cond(polar, lambda u, v, _: jnp.concatenate([u, v], axis=1), elsewhere, moved_u, moved_v, moved_offsets)
    moved = lax.ppermute(moved, "lat", inward)
    pieces = lax.cond(polar, swapped, lambda x: x, pieces)
    return joined(ids, pieces, moved, other, cols, rows).reshape(3, cols, rows, lev)


def solution(mesh):
    placed = (P(None, "lon", "lat", None), P("lat"))
    return jax.shard_map(
        body, mesh=mesh, in_specs=placed, out_specs=P(None, "lon", "lat", None), check_vma=False
    )
```

```python
import functools

import jax
import jax.numpy as jnp
import numpy as np
from jax import lax
from jax.experimental import pallas as pl
from jax.experimental.pallas import tpu as pltpu
from jax.sharding import PartitionSpec as P

SUBSTEPS = 2
HALO = 1 + 2 * SUBSTEPS
ADV = 0.5
SOUND = 0.8
CAP = 2.0
LEAD = 16
GROUP = 8
UNROLL = 2
PACK = 3
MIB = 1024 * 1024

f32 = jnp.float32
bf16 = jnp.bfloat16


def params(mib):
    return pltpu.CompilerParams(vmem_limit_bytes=mib * MIB)


def vmem():
    return pl.BlockSpec(memory_space=pltpu.VMEM)


def smem():
    return pl.BlockSpec(memory_space=pltpu.SMEM)


def edge_row(d):
    return jnp.where(d < 4, d, d + 8)


def inner_row(d):
    return d + 4


EDGE = [d if d < 4 else d + 8 for d in range(GROUP)]
INNER = [d + 4 for d in range(GROUP)]


def padded(cols):
    return -(-cols // 8) * 8


def window(cols):
    return -(-(8 + cols + HALO) // 8) * 8


def cost(micros):
    return pl.CostEstimate(flops=0, bytes_accessed=int(micros * 3.69e6), transcendentals=0)


def any_space():
    return pl.BlockSpec(memory_space=pltpu.MemorySpace.HBM)


def split_kernel(cols, rows, x_ref, _, __, planes_ref, north_ref, south_ref, hold, P, sem, out_sem):
    count = HALO - 1
    loads = [pltpu.make_async_copy(x_ref.at[c], hold.at[c], sem.at[c]) for c in range(3)]
    for copy in loads:
        copy.start()
    outs = []
    for c in range(3):
        loads[c].wait()
        for r in range(rows):
            P[c, r, pl.ds(8, cols)] = hold[c, pl.ds(r, cols, stride=rows), :]
        mine = [
            (P.at[c, pl.ds(0, count)], north_ref.at[pl.ds(count * c, count)]),
            (P.at[c, pl.ds(rows - count, count)], south_ref.at[pl.ds(count * c, count)]),
            (P.at[c], planes_ref.at[c]),
        ]
        if c == 2:
            mine.append((P.at[c, pl.ds(count, 1)], north_ref.at[pl.ds(3 * count, 1)]))
            mine.append((P.at[c, pl.ds(rows - HALO, 1)], south_ref.at[pl.ds(3 * count, 1)]))
        for s, d in mine:
            outs.append(pltpu.make_async_copy(s, d, out_sem.at[len(outs)]))
            outs[-1].start()
    for copy in outs:
        copy.wait()


def split_planes(flat, after, cols, rows):
    lev = flat.shape[-1]
    wide = window(cols)
    edge = jax.ShapeDtypeStruct((3 * (HALO - 1) + 1, wide, lev), f32)
    planes = (3, rows, wide, lev)
    return pl.pallas_call(
        functools.partial(split_kernel, cols, rows),
        in_specs=[any_space()] * 3,
        out_specs=[any_space()] * 3,
        out_shape=[jax.ShapeDtypeStruct(planes, f32), edge, edge],
        scratch_shapes=[
            pltpu.VMEM(flat.shape, f32),
            pltpu.VMEM(planes, f32),
            pltpu.SemaphoreType.DMA((3,)),
            pltpu.SemaphoreType.DMA((11,)),
        ],
        compiler_params=params(60),
    )(flat, *after)


def column_kernel(cols, rows, west_ref, east_ref, _, __, north_ref, south_ref, W, E, sem, out_sem):
    at = (8 + cols) // 8 * 8
    off = 8 + cols - at
    ends = ((north_ref, 0), (south_ref, 1))
    loads = [pltpu.make_async_copy(ref.at[:, pl.ds(at, 16)], E.at[k], sem.at[k]) for ref, k in ends]
    for copy in loads:
        copy.start()
    for k, (base, last) in enumerate(((0, HALO - 1), (rows - HALO + 1, rows - HALO))):
        planes = [(c, base + j) for c in range(3) for j in range(HALO - 1)] + [(2, last)]
        for n, (c, r) in enumerate(planes):
            W[k, n, pl.ds(8 - HALO, HALO)] = west_ref[c, pl.ds(r, HALO, stride=rows), :]
        loads[k].wait()
        for n, (c, r) in enumerate(planes):
            E[k, n, pl.ds(off, HALO)] = east_ref[c, pl.ds(r, HALO, stride=rows), :]
    outs = [pltpu.make_async_copy(E.at[k], ref.at[:, pl.ds(at, 16)], sem.at[k]) for ref, k in ends]
    outs += [pltpu.make_async_copy(W.at[k], ref.at[:, pl.ds(0, 8)], out_sem.at[k]) for ref, k in ends]
    for copy in outs:
        copy.start()
    for copy in outs:
        copy.wait()


def with_columns(west, east_, north, south, cols, rows):
    count, _, lev = north.shape
    return pl.pallas_call(
        functools.partial(column_kernel, cols, rows),
        in_specs=[vmem(), vmem(), any_space(), any_space()],
        out_specs=[any_space()] * 2,
        out_shape=[jax.ShapeDtypeStruct(north.shape, f32)] * 2,
        scratch_shapes=[
            pltpu.VMEM((2, count, 8, lev), f32),
            pltpu.VMEM((2, count, 16, lev), f32),
            pltpu.SemaphoreType.DMA((2,)),
            pltpu.SemaphoreType.DMA((2,)),
        ],
        input_output_aliases={2: 0, 3: 1},
        compiler_params=params(4),
    )(west, east_, north, south)


def east(W, r):
    cols = W.shape[1] - 16
    return W[r, pl.ds(9, cols)] - W[r, pl.ds(7, cols)]


def stage_steps(metric_ref, base, U, V, T, A, B, C, keep):
    mid = pl.ds(8, U.shape[1] - 16)

    def metric(i):
        return metric_ref[i + (HALO - base)]

    def advect(i, fields=None):
        mu = metric(i) * (0.5 * ADV) * U[i, mid]
        nv = (0.5 * ADV) * V[i, mid]
        for W, out in fields or ((U, A), (V, B), (T, C)):
            out[i, mid] = W[i, mid] - (mu * east(W, i) + nv * (W[i + 1, mid] - W[i - 1, mid]))

    def advect_theta(i):
        advect(i, ((T, C),))

    def wind_u(i):
        A[i, mid] = A[i, mid] - (metric(i) * (0.5 * SOUND)) * east(C, i)

    def wind_v(i):
        B[i, mid] = keep(i, B[i, mid] - (0.5 * SOUND) * (C[i + 1, mid] - C[i - 1, mid]))

    def theta(i):
        m = metric(i) * (0.5 * SOUND)
        C[i, mid] = keep(i, C[i, mid] - (m * east(A, i) + (0.5 * SOUND) * (B[i + 1, mid] - B[i - 1, mid])))

    return advect, advect_theta, wind_u, wind_v, theta


def sweep(fn, *spans):
    for lo, hi in spans:

        def step(i, carry):
            fn(i)
            return carry

        lax.fori_loop(lo, hi, step, 0, unroll=UNROLL)


def inner_kernel(
    cols, rows, metric_ref, planes_ref, west_ref, east_ref, off_ref, _, u_ref, v_ref, theta_ref, rim_ref, raw_ref, *scratch
):
    U, V, T, A, B, C, sem, out_sem = scratch
    own = slice(LEAD, LEAD + cols)
    wide = pl.ds(LEAD - 8, window(cols))
    loads = [pltpu.make_async_copy(planes_ref.at[c], W.at[:, wide], sem.at[c]) for c, W in enumerate((U, V, T))]
    for copy in loads:
        copy.start()
    outs = []
    for c, W in enumerate((U, V, T)):
        loads[c].wait()

        for r in range(rows):
            W[r, pl.ds(LEAD - HALO, HALO)] = west_ref[c, pl.ds(r, HALO, stride=rows), :]
            W[r, pl.ds(LEAD + cols, HALO)] = east_ref[c, pl.ds(r, HALO, stride=rows), :]
        for k, at in ((0, 0), (1, rows - 2)):
            outs.append((W.at[pl.ds(at, 2), wide], raw_ref.at[c, pl.ds(2 * k, 2)]))
    advect, _, wind_u, wind_v, theta = stage_steps(metric_ref, 0, U, V, T, A, B, C, lambda r, x: x)
    sweep(advect, (1, rows - 1))
    sweep(wind_u, (1, rows - 1))
    sweep(wind_v, (2, rows - 2))
    sweep(theta, (3, rows - 3))
    sweep(wind_u, (3, rows - 3))
    sweep(wind_v, (4, rows - 4))
    sweep(theta, (5, rows - 5))
    for c, W in enumerate((A, B, C)):
        for k, at in ((0, 1), (1, rows - 6)):
            outs.append((W.at[pl.ds(at, 5), wide], rim_ref.at[c, pl.ds(5 * k, 5)]))
    outs = [pltpu.make_async_copy(a, b, out_sem.at[i]) for i, (a, b) in enumerate(outs)]
    for copy in outs:
        copy.start()
    pad = padded(cols)
    for d in range(GROUP):
        u_ref[d, pl.ds(0, cols)] = A[INNER[d], own]
        u_ref[d, pl.ds(cols, PACK)] = off_ref[PACK * d : PACK * (d + 1)]
        v_ref[d, pl.ds(0, cols)] = B[INNER[d], own]
        theta_ref[d, pl.ds(0, cols)] = C[INNER[d], own]
    for copy in outs:
        copy.wait()


def inner_rows(metric, planes, west, east_, offsets, after, cols, rows):
    lev = planes.shape[-1]
    pad = padded(cols)
    wide = window(cols)
    shapes = [(GROUP, pad, lev)] * 3 + [(3, 10, wide, lev), (3, 4, wide, lev)]
    return pl.pallas_call(
        functools.partial(inner_kernel, cols, rows),
        in_specs=[smem(), any_space(), vmem(), vmem(), vmem(), any_space()],
        out_specs=[vmem()] * 3 + [any_space()] * 2,
        out_shape=[jax.ShapeDtypeStruct(s, f32) for s in shapes],
        scratch_shapes=[pltpu.VMEM((rows, LEAD + wide, lev), f32)] * 6
        + [pltpu.SemaphoreType.DMA((3,)), pltpu.SemaphoreType.DMA((12,))],
        compiler_params=params(60),
        cost_estimate=cost(9),
    )(metric, planes, west, east_, offsets, after)


def edge_kernel(
    cols, rows, ids_ref, metric_ref, raw_ref, rim_ref, hn_ref, hs_ref, u_ref, v_ref, theta_ref, _, send_ref, out_ref, *scratch
):
    U, V, T, A, B, C, hold, moved, sem, move_sem, out_sem = scratch
    own = slice(LEAD, LEAD + cols)
    wide = pl.ds(LEAD - 8, window(cols))
    pad = padded(cols)
    count = HALO - 1
    loads = []
    for c, W in enumerate((U, V, T)):
        loads.append((hn_ref.at[pl.ds(count * c, count)], W.at[pl.ds(1, count), wide]))
        loads.append((hs_ref.at[pl.ds(count * c, count)], W.at[pl.ds(HALO + rows, count), wide]))
        loads.append((raw_ref.at[c, pl.ds(0, 2)], W.at[pl.ds(HALO, 2), wide]))
        loads.append((raw_ref.at[c, pl.ds(2, 2)], W.at[pl.ds(HALO + rows - 2, 2), wide]))
    loads.append((hn_ref.at[pl.ds(3 * count, 1)], T.at[pl.ds(0, 1), wide]))
    loads.append((hs_ref.at[pl.ds(3 * count, 1)], T.at[pl.ds(2 * HALO + rows - 1, 1), wide]))
    for c, W in enumerate((A, B, C)):
        loads.append((rim_ref.at[c, pl.ds(0, 5)], W.at[pl.ds(HALO + 1, 5), wide]))
        loads.append((rim_ref.at[c, pl.ds(5, 5)], W.at[pl.ds(HALO + rows - 6, 5), wide]))
    loads = [pltpu.make_async_copy(a, b, sem.at[i]) for i, (a, b) in enumerate(loads)]
    for copy in loads:
        copy.start()
    for copy in loads:
        copy.wait()
    has_north = jnp.where(ids_ref[1] > 0, 1.0, 0.0)
    has_south = jnp.where(ids_ref[2] > 0, 1.0, 0.0)

    def keep(i, x):
        return x * jnp.where(i >= HALO + rows, has_south, jnp.where(i < HALO, has_north, 1.0))

    advect, advect_theta, wind_u, wind_v, theta = stage_steps(metric_ref, HALO, U, V, T, A, B, C, keep)

    def ends(fn, lo, hi):
        sweep(fn, (HALO + lo, HALO + hi), (HALO + rows - hi, HALO + rows - lo))

    ends(advect, -3, 1)
    ends(advect_theta, -4, -3)
    ends(wind_u, -2, 1)
    ends(wind_v, -3, 2)
    ends(theta, -2, 3)
    ends(wind_u, 0, 3)
    ends(wind_v, -1, 4)
    ends(theta, 0, 5)

    @pl.when(ids_ref[3] != 0)
    def _():
        inside = pltpu.make_async_copy(
            theta_ref.at[pl.ds(1, GROUP - 2)], send_ref.at[pl.ds(1, GROUP - 2), pl.ds(3 * pad, pad)], move_sem.at[0]
        )
        inside.start()
        for d in range(GROUP):
            for c, W in enumerate((A, B, C)):
                send_ref[d, pl.ds(c * pad, cols)] = W[EDGE[d] + HALO, own]
        for d in (0, GROUP - 1):
            send_ref[d, pl.ds(3 * pad, cols)] = C[INNER[d] + HALO, own]
        inside.wait()

    @pl.when(ids_ref[3] == 0)
    def _():
        inside = [
            pltpu.make_async_copy(ref, moved.at[:, pl.ds(c * pad, pad)], move_sem.at[c])
            for c, ref in enumerate((u_ref, v_ref, theta_ref))
        ]
        for copy in inside:
            copy.start()
        for copy in inside:
            copy.wait()
        outs = [pltpu.make_async_copy(hold.at[c], out_ref.at[c], out_sem.at[c]) for c in range(3)]
        for c, W in enumerate((A, B, C)):
            for d in range(GROUP):
                hold[c, pl.ds(EDGE[d], cols, stride=rows), :] = W[EDGE[d] + HALO, own]
                if c == 2 and d in (0, GROUP - 1):
                    value = C[INNER[d] + HALO, own]
                else:
                    value = moved[d, pl.ds(c * pad, cols)]
                hold[c, pl.ds(INNER[d], cols, stride=rows), :] = value
            outs[c].start()
        for out in outs:
            out.wait()


def edge_rows(ids, metric, raw, rim, hn, hs, inner, after, cols, rows):
    lev = raw.shape[-1]
    pad = padded(cols)
    whole = (3, cols * rows, lev)
    return pl.pallas_call(
        functools.partial(edge_kernel, cols, rows),
        in_specs=[smem(), smem()] + [any_space()] * 8,
        out_specs=[vmem(), any_space()],
        out_shape=[jax.ShapeDtypeStruct((GROUP, 4 * pad, lev), f32), jax.ShapeDtypeStruct(whole, f32)],
        scratch_shapes=[pltpu.VMEM((rows + 2 * HALO, LEAD + window(cols), lev), f32)] * 6
        + [pltpu.VMEM(whole, f32), pltpu.VMEM((GROUP, 3 * pad, lev), f32)]
        + [pltpu.SemaphoreType.DMA((n,)) for n in (20, 3, 3)],
        compiler_params=params(60),
        cost_estimate=cost(8),
    )(ids, metric, raw, rim, hn, hs, *inner, after)


def offset_tables(length):
    half = length // 2
    pad = -(-half // 256) * 256
    n = np.arange(2 * pad) - pad
    tables = []
    for first in (0, 1):
        wave = np.arange(first, half + 1, 2)
        weight = np.where((wave == 0) | (wave == half), 1.0, 2.0) / length
        angle = (wave[:, None] * n[None, :]) % length * (2.0 * np.pi / length)
        tables.append((wave, (np.cos(angle) * weight[:, None]).astype(np.float32)))
    return tables


def offset_values(limits, length):
    values = []
    for wave, table in offset_tables(length):
        w = jnp.asarray(wave, f32)
        lim = limits[:, None]
        factor = jnp.where(w[None, :] <= lim, 1.0, (lim / jnp.maximum(w, 1.0)[None, :]) ** 2)
        values.append(jnp.dot(factor, jnp.asarray(table), precision=lax.Precision.HIGHEST, preferred_element_type=f32))
    return jnp.stack(values, axis=1)[:, :, None, :]


def skew(p, store):
    width = p.shape[-1]
    line = lax.broadcasted_iota(jnp.int32, (8, width), 0)
    x = jnp.broadcast_to(p, (8, width))
    for bit in range(3):
        x = jnp.where((line & (1 << bit)) != 0, pltpu.roll(x, 1 << bit, 1), x)
    for pair in range(8):
        two = [pltpu.roll(x, 8 * g, 1)[:, 128:] if g else x[:, 128:] for g in (2 * pair, 2 * pair + 1)]
        y = jnp.concatenate(two, axis=0)
        hi = y.astype(bf16)
        store(16 * pair, hi, (y - hi.astype(f32)).astype(bf16))


def unpack_kernel(length, x_ref, _, hi_ref, lo_ref):
    cols = length // GROUP
    lines = [x_ref[d, cols + j : cols + j + 1] for d in range(GROUP) for j in range(PACK)]
    half = len(lines) // 2
    for e in range(2):

        def store(at, hi, lo, e=e):
            hi_ref[0, e, at : at + 16] = hi
            lo_ref[0, e, at : at + 16] = lo

        skew(jnp.concatenate(lines[e * half : (e + 1) * half], axis=1), store)


def unpacked(x, length, after):
    width = GROUP * PACK * x.shape[-1] // 2
    out = jax.ShapeDtypeStruct((1, 2, 128, width - 128), bf16)
    return pl.pallas_call(
        functools.partial(unpack_kernel, length),
        in_specs=[vmem(), any_space()],
        out_specs=[vmem()] * 2,
        out_shape=[out, out],
        compiler_params=params(16),
    )(x, after)


def skew_kernel(p_ref, _, hi_ref, lo_ref):
    rows, parts, _, width = p_ref.shape
    for r in range(rows):
        for e in range(parts):

            def store(at, hi, lo, r=r, e=e):
                hi_ref[r, e, at : at + 16] = hi
                lo_ref[r, e, at : at + 16] = lo

            skew(p_ref[r, e], store)


def skewed(values, after):
    rows, parts, _, width = values.shape
    out = jax.ShapeDtypeStruct((rows, parts, 128, width - 128), bf16)
    return pl.pallas_call(
        skew_kernel,
        in_specs=[vmem(), any_space()],
        out_specs=[vmem()] * 2,
        out_shape=[out, out],
        compiler_params=params(16),
    )(values, after)


def filter_kernel(groups, cols, hi_ref, lo_ref, x_ref, _, y_ref, S, D, Y, Z):
    quarter = GROUP // 2
    size = S.shape[0]
    lev = x_ref.shape[-1]
    pad = padded(cols)
    units = [u for _, members in groups for u in members]
    S[quarter * cols :] = jnp.zeros((size - quarter * cols, S.shape[1]), f32)
    D[quarter * cols :] = jnp.zeros((size - quarter * cols, S.shape[1]), f32)
    for b in range(quarter):
        at = slice(b * cols, (b + 1) * cols)
        for i, u in enumerate(units):
            lanes = slice(i * lev, (i + 1) * lev)
            one = x_ref[b, pl.ds(u * pad, cols)]
            two = x_ref[b + quarter, pl.ds(u * pad, cols)]
            S[at, lanes] = one + two
            D[at, lanes] = one - two
    tall = size // 128
    first = 0
    for row, members in groups:
        lanes = slice(first * lev, (first + len(members)) * lev)
        first += len(members)

        def matrix(ref, e, row=row):
            starts = [(tall - 1 - b) * 128 for b in range(tall)]
            return jnp.concatenate([ref[row, e, :, st : st + size] for st in starts], axis=0)

        for e, (src, dst) in enumerate(((S, Y), (D, Z))):
            x = src[:, lanes]
            xh = x.astype(bf16)
            xl = (x - xh.astype(f32)).astype(bf16)
            mh = matrix(hi_ref, e)
            left = jnp.concatenate([mh, mh, matrix(lo_ref, e)], axis=1)
            right = jnp.concatenate([xh, xl, xh], axis=0)
            dst[:, lanes] = jnp.dot(left, right, preferred_element_type=f32)
    for b in range(quarter):
        at = slice(b * cols, (b + 1) * cols)
        for i, u in enumerate(units):
            lanes = slice(i * lev, (i + 1) * lev)
            y = Y[at, lanes]
            z = Z[at, lanes]
            y_ref[b, pl.ds(u * pad, cols)] = y + z
            y_ref[b + quarter, pl.ds(u * pad, cols)] = y - z


def filtered(groups, hi, lo, whole, after, cols):
    _, tall, lev = whole.shape
    count = sum(len(members) for _, members in groups)
    work = pltpu.VMEM((hi.shape[-1] - 128 * 5, count * lev), f32)
    return pl.pallas_call(
        functools.partial(filter_kernel, groups, cols),
        in_specs=[vmem()] * 3 + [any_space()],
        out_specs=vmem(),
        out_shape=jax.ShapeDtypeStruct(whole.shape, f32),
        scratch_shapes=[work] * 4,
        compiler_params=params(28),
    )(hi, lo, whole, after)


def join_kernel(cols, rows, ids_ref, y_ref, u_ref, v_ref, _, out_ref, held, moved, result, sem, out_sem):
    @pl.when(ids_ref[3] != 0)
    def _():
        pad = padded(cols)
        copies = [pltpu.make_async_copy(y_ref.at[:, pl.ds(u * pad, pad)], held.at[u], sem.at[u]) for u in range(4)]
        copies += [pltpu.make_async_copy(ref, moved.at[u], sem.at[4 + u]) for u, ref in enumerate((u_ref, v_ref))]
        outs = [pltpu.make_async_copy(result.at[c], out_ref.at[c], out_sem.at[c]) for c in range(3)]
        for copy in copies:
            copy.start()
        for c, inner, wait in ((0, moved.at[0], 4), (1, moved.at[1], 5), (2, held.at[3], 3)):
            copies[c].wait()
            copies[wait].wait()
            for d in range(GROUP):
                result[c, pl.ds(EDGE[d], cols, stride=rows), :] = held[c, d, 0:cols]
                result[c, pl.ds(INNER[d], cols, stride=rows), :] = inner[d, 0:cols]
            outs[c].start()
        for c in range(3):
            outs[c].wait()


def joined(ids, whole, moved_u, moved_v, other, cols, rows):
    lev = whole.shape[-1]
    pad = padded(cols)
    return pl.pallas_call(
        functools.partial(join_kernel, cols, rows),
        in_specs=[smem()] + [any_space()] * 4,
        out_specs=any_space(),
        out_shape=jax.ShapeDtypeStruct(other.shape, f32),
        scratch_shapes=[
            pltpu.VMEM((4, GROUP, pad, lev), f32),
            pltpu.VMEM((2, GROUP, pad, lev), f32),
            pltpu.VMEM(other.shape, f32),
            pltpu.SemaphoreType.DMA((6,)),
            pltpu.SemaphoreType.DMA((3,)),
        ],
        input_output_aliases={4: 0},
        compiler_params=params(16),
    )(ids, whole, moved_u, moved_v, other)


def tie_kernel(x_ref, _, out_ref):
    pass


def tied(x, y):
    return pl.pallas_call(
        tie_kernel,
        in_specs=[any_space()] * 2,
        out_specs=any_space(),
        out_shape=jax.ShapeDtypeStruct(x.shape, x.dtype),
        input_output_aliases={0: 0},
        compiler_params=params(1),
    )(x, y)


def hollow_kernel(out_ref):
    pass


def hollow(x):
    return pl.pallas_call(
        hollow_kernel,
        out_specs=any_space(),
        out_shape=jax.ShapeDtypeStruct(x.shape, x.dtype),
        compiler_params=params(1),
    )()


def swapped(x):
    return lax.all_to_all(x, "lon", split_axis=0, concat_axis=0, tiled=True)


def body(state, cutoffs):
    lat_count = lax.axis_size("lat")
    lon_count = lax.axis_size("lon")
    _, cols, rows, lev = state.shape
    total_lat = rows * lat_count
    total_lon = cols * lon_count
    band = lax.axis_index("lat")
    me = lax.axis_index("lon")
    quarter = lat_count // 4
    polar = (band < quarter) | (band >= lat_count - quarter)
    ids = jnp.stack([me, band, lat_count - 1 - band, polar.astype(jnp.int32)]).astype(jnp.int32)

    up = [(i, i + 1) for i in range(lat_count - 1)]
    down = [(j, i) for i, j in up]
    right = [(i, (i + 1) % lon_count) for i in range(lon_count)]
    left = [(j, i) for i, j in right]

    flat = state.reshape(3, cols * rows, lev)
    last = state[:, cols - HALO :].reshape(3, HALO * rows, lev)
    first = state[:, :HALO].reshape(3, HALO * rows, lev)
    west = lax.ppermute(last, "lon", right)
    east_ = lax.ppermute(first, "lon", left)
    outward = [(b, b + quarter) for b in range(quarter)]
    outward += [(b, b - quarter) for b in range(lat_count - quarter, lat_count)]
    inward = [(j, i) for i, j in outward]
    near = band * rows - HALO + jnp.arange(rows + 2 * HALO, dtype=jnp.int32)
    latitude = (-90.0 + (near.astype(f32) + 0.5) * (180.0 / total_lat)) * (jnp.pi / 180.0)
    metric = 1.0 / jnp.maximum(jnp.cos(latitude), 1.0 / CAP)

    wanted = jnp.stack([edge_row(me), inner_row(me)])
    chosen = wanted[:, None] == jnp.arange(rows, dtype=jnp.int32)[None, :]
    picked = jnp.sum(jnp.where(chosen, cutoffs.astype(f32)[None, :], 0.0), axis=1)
    offsets = offset_values(picked, total_lon)
    token = jnp.zeros((8, lev), f32)
    packed = offsets[1].reshape(GROUP * PACK, lev)
    hi, lo = skewed(offsets, token)
    planes, own_north, own_south = split_planes(flat, (last, first), cols, rows)
    send_north, send_south = with_columns(west, east_, own_north, own_south, cols, rows)
    halo_north = lax.ppermute(send_south, "lat", up)
    halo_south = lax.ppermute(send_north, "lat", down)

    u, v, theta, rim, raw = inner_rows(metric, planes, west, east_, packed, send_north, cols, rows)
    moved_u = lax.ppermute(u, "lat", outward)
    moved_v = lax.ppermute(v, "lat", outward)
    pieces, other = edge_rows(ids, metric, raw, rim, halo_north, halo_south, (u, v, theta), lo, cols, rows)

    def elsewhere(x, first, after):
        hi, lo = unpacked(first, total_lon, after)
        return swapped(filtered(((0, (0,)),), hi, lo, swapped(x), after, cols))

    def idle(x, *_):
        return hollow(x)

    def near_pole(x, after):
        return swapped(filtered(((0, (0, 1, 2)), (1, (3,))), hi, lo, x, after, cols))

    def same(x, *_):
        return x

    whole = lax.cond(polar, swapped, same, pieces)
    back_u = lax.cond(polar, idle, elsewhere, moved_u, moved_u, tied(token, whole))
    moved_back_u = lax.ppermute(back_u, "lat", inward)
    back_v = lax.cond(polar, idle, elsewhere, moved_v, moved_u, tied(token, whole))
    moved_back_v = lax.ppermute(back_v, "lat", inward)
    pieces = lax.cond(polar, near_pole, same, whole, tied(token, back_v))
    return joined(ids, pieces, moved_back_u, moved_back_v, other, cols, rows).reshape(3, cols, rows, lev)


def solution(mesh):
    placed = (P(None, "lon", "lat", None), P("lat"))
    return jax.shard_map(
        body, mesh=mesh, in_specs=placed, out_specs=P(None, "lon", "lat", None), check_vma=False
    )
```

```python
import functools

import jax
import jax.numpy as jnp
import numpy as np
from jax import lax
from jax.experimental import pallas as pl
from jax.experimental.pallas import tpu as pltpu
from jax.sharding import PartitionSpec as P

SUBSTEPS = 2
HALO = 1 + 2 * SUBSTEPS
ADV = 0.5
SOUND = 0.8
CAP = 2.0
LEAD = 16
GROUP = 8
UNROLL = 2
PACK = 3
MIB = 1024 * 1024

f32 = jnp.float32
bf16 = jnp.bfloat16


def params(mib):
    return pltpu.CompilerParams(vmem_limit_bytes=mib * MIB)


def vmem():
    return pl.BlockSpec(memory_space=pltpu.VMEM)


def smem():
    return pl.BlockSpec(memory_space=pltpu.SMEM)


def edge_row(d):
    return jnp.where(d < 4, d, d + 8)


def inner_row(d):
    return d + 4


EDGE = [d if d < 4 else d + 8 for d in range(GROUP)]
INNER = [d + 4 for d in range(GROUP)]


def padded(cols):
    return -(-cols // 8) * 8


def window(cols):
    return -(-(8 + cols + HALO) // 8) * 8


def cost(micros):
    return pl.CostEstimate(flops=0, bytes_accessed=int(micros * 3.69e6), transcendentals=0)


def any_space():
    return pl.BlockSpec(memory_space=pltpu.MemorySpace.HBM)


def split_kernel(cols, rows, x_ref, _, __, planes_ref, north_ref, south_ref, hold, P, sem, out_sem):
    count = HALO - 1
    loads = [pltpu.make_async_copy(x_ref.at[c], hold.at[c], sem.at[c]) for c in range(3)]
    for copy in loads:
        copy.start()
    outs = []
    for c in range(3):
        loads[c].wait()
        for r in range(rows):
            P[c, r, pl.ds(8, cols)] = hold[c, pl.ds(r, cols, stride=rows), :]
        mine = [
            (P.at[c, pl.ds(0, count)], north_ref.at[pl.ds(count * c, count)]),
            (P.at[c, pl.ds(rows - count, count)], south_ref.at[pl.ds(count * c, count)]),
            (P.at[c], planes_ref.at[c]),
        ]
        if c == 2:
            mine.append((P.at[c, pl.ds(count, 1)], north_ref.at[pl.ds(3 * count, 1)]))
            mine.append((P.at[c, pl.ds(rows - HALO, 1)], south_ref.at[pl.ds(3 * count, 1)]))
        for s, d in mine:
            outs.append(pltpu.make_async_copy(s, d, out_sem.at[len(outs)]))
            outs[-1].start()
    for copy in outs:
        copy.wait()


def split_planes(flat, after, cols, rows):
    lev = flat.shape[-1]
    wide = window(cols)
    edge = jax.ShapeDtypeStruct((3 * (HALO - 1) + 1, wide, lev), f32)
    planes = (3, rows, wide, lev)
    return pl.pallas_call(
        functools.partial(split_kernel, cols, rows),
        in_specs=[any_space()] * 3,
        out_specs=[any_space()] * 3,
        out_shape=[jax.ShapeDtypeStruct(planes, f32), edge, edge],
        scratch_shapes=[
            pltpu.VMEM(flat.shape, f32),
            pltpu.VMEM(planes, f32),
            pltpu.SemaphoreType.DMA((3,)),
            pltpu.SemaphoreType.DMA((11,)),
        ],
        compiler_params=params(60),
    )(flat, *after)


def column_kernel(cols, rows, west_ref, east_ref, _, __, north_ref, south_ref, W, E, sem, out_sem):
    at = (8 + cols) // 8 * 8
    off = 8 + cols - at
    ends = ((north_ref, 0), (south_ref, 1))
    loads = [pltpu.make_async_copy(ref.at[:, pl.ds(at, 16)], E.at[k], sem.at[k]) for ref, k in ends]
    for copy in loads:
        copy.start()
    for k, (base, last) in enumerate(((0, HALO - 1), (rows - HALO + 1, rows - HALO))):
        planes = [(c, base + j) for c in range(3) for j in range(HALO - 1)] + [(2, last)]
        for n, (c, r) in enumerate(planes):
            W[k, n, pl.ds(8 - HALO, HALO)] = west_ref[c, pl.ds(r, HALO, stride=rows), :]
        loads[k].wait()
        for n, (c, r) in enumerate(planes):
            E[k, n, pl.ds(off, HALO)] = east_ref[c, pl.ds(r, HALO, stride=rows), :]
    outs = [pltpu.make_async_copy(E.at[k], ref.at[:, pl.ds(at, 16)], sem.at[k]) for ref, k in ends]
    outs += [pltpu.make_async_copy(W.at[k], ref.at[:, pl.ds(0, 8)], out_sem.at[k]) for ref, k in ends]
    for copy in outs:
        copy.start()
    for copy in outs:
        copy.wait()


def with_columns(west, east_, north, south, cols, rows):
    count, _, lev = north.shape
    return pl.pallas_call(
        functools.partial(column_kernel, cols, rows),
        in_specs=[vmem(), vmem(), any_space(), any_space()],
        out_specs=[any_space()] * 2,
        out_shape=[jax.ShapeDtypeStruct(north.shape, f32)] * 2,
        scratch_shapes=[
            pltpu.VMEM((2, count, 8, lev), f32),
            pltpu.VMEM((2, count, 16, lev), f32),
            pltpu.SemaphoreType.DMA((2,)),
            pltpu.SemaphoreType.DMA((2,)),
        ],
        input_output_aliases={2: 0, 3: 1},
        compiler_params=params(4),
    )(west, east_, north, south)


def east(W, r):
    cols = W.shape[1] - 16
    return W[r, pl.ds(9, cols)] - W[r, pl.ds(7, cols)]


def stage_steps(metric_ref, base, U, V, T, A, B, C, keep):
    mid = pl.ds(8, U.shape[1] - 16)

    def metric(i):
        return metric_ref[i + (HALO - base)]

    def advect(i, fields=None):
        mu = metric(i) * (0.5 * ADV) * U[i, mid]
        nv = (0.5 * ADV) * V[i, mid]
        for W, out in fields or ((U, A), (V, B), (T, C)):
            out[i, mid] = W[i, mid] - (mu * east(W, i) + nv * (W[i + 1, mid] - W[i - 1, mid]))

    def advect_theta(i):
        advect(i, ((T, C),))

    def wind_u(i):
        A[i, mid] = A[i, mid] - (metric(i) * (0.5 * SOUND)) * east(C, i)

    def wind_v(i):
        B[i, mid] = keep(i, B[i, mid] - (0.5 * SOUND) * (C[i + 1, mid] - C[i - 1, mid]))

    def theta(i):
        m = metric(i) * (0.5 * SOUND)
        C[i, mid] = keep(i, C[i, mid] - (m * east(A, i) + (0.5 * SOUND) * (B[i + 1, mid] - B[i - 1, mid])))

    return advect, advect_theta, wind_u, wind_v, theta


def sweep(fn, *spans):
    for lo, hi in spans:

        def step(i, carry):
            fn(i)
            return carry

        lax.fori_loop(lo, hi, step, 0, unroll=UNROLL)


def inner_kernel(
    cols, rows, metric_ref, planes_ref, west_ref, east_ref, off_ref, _, u_ref, v_ref, theta_ref, rim_ref, raw_ref, *scratch
):
    U, V, T, A, B, C, sem, out_sem = scratch
    own = slice(LEAD, LEAD + cols)
    wide = pl.ds(LEAD - 8, window(cols))
    loads = [pltpu.make_async_copy(planes_ref.at[c], W.at[:, wide], sem.at[c]) for c, W in enumerate((U, V, T))]
    for copy in loads:
        copy.start()
    outs = []
    for c, W in enumerate((U, V, T)):
        loads[c].wait()

        for r in range(rows):
            W[r, pl.ds(LEAD - HALO, HALO)] = west_ref[c, pl.ds(r, HALO, stride=rows), :]
            W[r, pl.ds(LEAD + cols, HALO)] = east_ref[c, pl.ds(r, HALO, stride=rows), :]
        for k, at in ((0, 0), (1, rows - 2)):
            outs.append((W.at[pl.ds(at, 2), wide], raw_ref.at[c, pl.ds(2 * k, 2)]))
    advect, _, wind_u, wind_v, theta = stage_steps(metric_ref, 0, U, V, T, A, B, C, lambda r, x: x)
    sweep(advect, (1, rows - 1))
    sweep(wind_u, (1, rows - 1))
    sweep(wind_v, (2, rows - 2))
    sweep(theta, (3, rows - 3))
    sweep(wind_u, (3, rows - 3))
    sweep(wind_v, (4, rows - 4))
    sweep(theta, (5, rows - 5))
    for c, W in enumerate((A, B, C)):
        for k, at in ((0, 1), (1, rows - 6)):
            outs.append((W.at[pl.ds(at, 5), wide], rim_ref.at[c, pl.ds(5 * k, 5)]))
    outs = [pltpu.make_async_copy(a, b, out_sem.at[i]) for i, (a, b) in enumerate(outs)]
    for copy in outs:
        copy.start()
    pad = padded(cols)
    for d in range(GROUP):
        u_ref[d, pl.ds(0, cols)] = A[INNER[d], own]
        u_ref[d, pl.ds(cols, PACK)] = off_ref[PACK * d : PACK * (d + 1)]
        v_ref[d, pl.ds(0, cols)] = B[INNER[d], own]
        theta_ref[d, pl.ds(0, cols)] = C[INNER[d], own]
    for copy in outs:
        copy.wait()


def inner_rows(metric, planes, west, east_, offsets, after, cols, rows):
    lev = planes.shape[-1]
    pad = padded(cols)
    wide = window(cols)
    shapes = [(GROUP, pad, lev)] * 3 + [(3, 10, wide, lev), (3, 4, wide, lev)]
    return pl.pallas_call(
        functools.partial(inner_kernel, cols, rows),
        in_specs=[smem(), any_space(), vmem(), vmem(), vmem(), any_space()],
        out_specs=[vmem()] * 3 + [any_space()] * 2,
        out_shape=[jax.ShapeDtypeStruct(s, f32) for s in shapes],
        scratch_shapes=[pltpu.VMEM((rows, LEAD + wide, lev), f32)] * 6
        + [pltpu.SemaphoreType.DMA((3,)), pltpu.SemaphoreType.DMA((12,))],
        compiler_params=params(60),
        cost_estimate=cost(9),
    )(metric, planes, west, east_, offsets, after)


def edge_kernel(cols, rows, near_pole, ids_ref, *refs):
    @pl.when((ids_ref[3] != 0) if near_pole else (ids_ref[3] == 0))
    def _():
        edge_steps(cols, rows, near_pole, ids_ref, *refs)


def edge_steps(
    cols, rows, near_pole, ids_ref, metric_ref, raw_ref, rim_ref, hn_ref, hs_ref, u_ref, v_ref, theta_ref, _, out_ref, *scratch
):
    U, V, T, A, B, C, sem, move_sem, *more = scratch
    own = slice(LEAD, LEAD + cols)
    wide = pl.ds(LEAD - 8, window(cols))
    pad = padded(cols)
    count = HALO - 1
    loads = []
    for c, W in enumerate((U, V, T)):
        loads.append((hn_ref.at[pl.ds(count * c, count)], W.at[pl.ds(1, count), wide]))
        loads.append((hs_ref.at[pl.ds(count * c, count)], W.at[pl.ds(HALO + rows, count), wide]))
        loads.append((raw_ref.at[c, pl.ds(0, 2)], W.at[pl.ds(HALO, 2), wide]))
        loads.append((raw_ref.at[c, pl.ds(2, 2)], W.at[pl.ds(HALO + rows - 2, 2), wide]))
    loads.append((hn_ref.at[pl.ds(3 * count, 1)], T.at[pl.ds(0, 1), wide]))
    loads.append((hs_ref.at[pl.ds(3 * count, 1)], T.at[pl.ds(2 * HALO + rows - 1, 1), wide]))
    for c, W in enumerate((A, B, C)):
        loads.append((rim_ref.at[c, pl.ds(0, 5)], W.at[pl.ds(HALO + 1, 5), wide]))
        loads.append((rim_ref.at[c, pl.ds(5, 5)], W.at[pl.ds(HALO + rows - 6, 5), wide]))
    loads = [pltpu.make_async_copy(a, b, sem.at[i]) for i, (a, b) in enumerate(loads)]
    for copy in loads:
        copy.start()
    for copy in loads[:14]:
        copy.wait()
    has_north = jnp.where(ids_ref[1] > 0, 1.0, 0.0)
    has_south = jnp.where(ids_ref[2] > 0, 1.0, 0.0)

    def keep(i, x):
        return x * jnp.where(i >= HALO + rows, has_south, jnp.where(i < HALO, has_north, 1.0))

    advect, advect_theta, wind_u, wind_v, theta = stage_steps(metric_ref, HALO, U, V, T, A, B, C, keep)

    def ends(fn, lo, hi):
        sweep(fn, (HALO + lo, HALO + hi), (HALO + rows - hi, HALO + rows - lo))

    ends(advect, -3, 1)
    ends(advect_theta, -4, -3)
    for copy in loads[14:]:
        copy.wait()
    ends(wind_u, -2, 1)
    ends(wind_v, -3, 2)
    ends(theta, -2, 3)
    ends(wind_u, 0, 3)
    ends(wind_v, -1, 4)
    ends(theta, 0, 5)

    if near_pole:
        inside = pltpu.make_async_copy(
            theta_ref.at[pl.ds(1, GROUP - 2)], out_ref.at[pl.ds(1, GROUP - 2), pl.ds(3 * pad, pad)], move_sem.at[0]
        )
        inside.start()
        for d in range(GROUP):
            for c, W in enumerate((A, B, C)):
                out_ref[d, pl.ds(c * pad, cols)] = W[EDGE[d] + HALO, own]
        for d in (0, GROUP - 1):
            out_ref[d, pl.ds(3 * pad, cols)] = C[INNER[d] + HALO, own]
        inside.wait()
    else:
        hold, moved, out_sem = more
        inside = [
            pltpu.make_async_copy(ref, moved.at[:, pl.ds(c * pad, pad)], move_sem.at[c])
            for c, ref in enumerate((u_ref, v_ref, theta_ref))
        ]
        for copy in inside:
            copy.start()
        for copy in inside:
            copy.wait()
        outs = [pltpu.make_async_copy(hold.at[c], out_ref.at[c], out_sem.at[c]) for c in range(3)]
        for c, W in enumerate((A, B, C)):
            for d in range(GROUP):
                hold[c, pl.ds(EDGE[d], cols, stride=rows), :] = W[EDGE[d] + HALO, own]
                if c == 2 and d in (0, GROUP - 1):
                    value = C[INNER[d] + HALO, own]
                else:
                    value = moved[d, pl.ds(c * pad, cols)]
                hold[c, pl.ds(INNER[d], cols, stride=rows), :] = value
            outs[c].start()
        for out in outs:
            out.wait()


def edge_rows(near_pole, ids, metric, raw, rim, hn, hs, inner, after, cols, rows):
    lev = raw.shape[-1]
    pad = padded(cols)
    whole = (3, cols * rows, lev)
    scratch = [pltpu.VMEM((rows + 2 * HALO, LEAD + window(cols), lev), f32)] * 6
    scratch += [pltpu.SemaphoreType.DMA((20,)), pltpu.SemaphoreType.DMA((3,))]
    if not near_pole:
        scratch += [pltpu.VMEM(whole, f32), pltpu.VMEM((GROUP, 3 * pad, lev), f32), pltpu.SemaphoreType.DMA((3,))]
    return pl.pallas_call(
        functools.partial(edge_kernel, cols, rows, near_pole),
        in_specs=[smem(), smem()] + [any_space()] * 8,
        out_specs=vmem() if near_pole else any_space(),
        out_shape=jax.ShapeDtypeStruct((GROUP, 4 * pad, lev) if near_pole else whole, f32),
        scratch_shapes=scratch,
        compiler_params=params(57 if near_pole else 60),
    )(ids, metric, raw, rim, hn, hs, *inner, after)


def offset_tables(length):
    half = length // 2
    pad = -(-half // 256) * 256
    n = np.arange(2 * pad) - pad
    tables = []
    for first in (0, 1):
        wave = np.arange(first, half + 1, 2)
        weight = np.where((wave == 0) | (wave == half), 1.0, 2.0) / length
        angle = (wave[:, None] * n[None, :]) % length * (2.0 * np.pi / length)
        tables.append((wave, (np.cos(angle) * weight[:, None]).astype(np.float32)))
    return tables


def offset_values(limits, length):
    values = []
    for wave, table in offset_tables(length):
        w = jnp.asarray(wave, f32)
        lim = limits[:, None]
        factor = jnp.where(w[None, :] <= lim, 1.0, (lim / jnp.maximum(w, 1.0)[None, :]) ** 2)
        values.append(jnp.dot(factor, jnp.asarray(table), precision=lax.Precision.HIGHEST, preferred_element_type=f32))
    return jnp.stack(values, axis=1)[:, :, None, :]


def skew(p, store):
    width = p.shape[-1]
    line = lax.broadcasted_iota(jnp.int32, (8, width), 0)
    x = jnp.broadcast_to(p, (8, width))
    for bit in range(3):
        x = jnp.where((line & (1 << bit)) != 0, pltpu.roll(x, 1 << bit, 1), x)
    for pair in range(8):
        two = [pltpu.roll(x, 8 * g, 1)[:, 128:] if g else x[:, 128:] for g in (2 * pair, 2 * pair + 1)]
        y = jnp.concatenate(two, axis=0)
        hi = y.astype(bf16)
        store(16 * pair, hi, (y - hi.astype(f32)).astype(bf16))


def unpack_kernel(length, x_ref, _, hi_ref, lo_ref):
    cols = length // GROUP
    lines = [x_ref[d, cols + j : cols + j + 1] for d in range(GROUP) for j in range(PACK)]
    half = len(lines) // 2
    for e in range(2):

        def store(at, hi, lo, e=e):
            hi_ref[0, e, at : at + 16] = hi
            lo_ref[0, e, at : at + 16] = lo

        skew(jnp.concatenate(lines[e * half : (e + 1) * half], axis=1), store)


def unpacked(x, length, after):
    width = GROUP * PACK * x.shape[-1] // 2
    out = jax.ShapeDtypeStruct((1, 2, 128, width - 128), bf16)
    return pl.pallas_call(
        functools.partial(unpack_kernel, length),
        in_specs=[vmem(), any_space()],
        out_specs=[vmem()] * 2,
        out_shape=[out, out],
        compiler_params=params(16),
    )(x, after)


def skew_kernel(p_ref, _, hi_ref, lo_ref):
    rows, parts, _, width = p_ref.shape
    for r in range(rows):
        for e in range(parts):

            def store(at, hi, lo, r=r, e=e):
                hi_ref[r, e, at : at + 16] = hi
                lo_ref[r, e, at : at + 16] = lo

            skew(p_ref[r, e], store)


def skewed(values, after):
    rows, parts, _, width = values.shape
    out = jax.ShapeDtypeStruct((rows, parts, 128, width - 128), bf16)
    return pl.pallas_call(
        skew_kernel,
        in_specs=[vmem(), any_space()],
        out_specs=[vmem()] * 2,
        out_shape=[out, out],
        compiler_params=params(16),
    )(values, after)


def filter_kernel(groups, cols, hi_ref, lo_ref, x_ref, _, y_ref, S, D, Y, Z):
    quarter = GROUP // 2
    size = S.shape[0]
    lev = x_ref.shape[-1]
    pad = padded(cols)
    units = [u for _, members in groups for u in members]
    S[quarter * cols :] = jnp.zeros((size - quarter * cols, S.shape[1]), f32)
    D[quarter * cols :] = jnp.zeros((size - quarter * cols, S.shape[1]), f32)
    for b in range(quarter):
        at = slice(b * cols, (b + 1) * cols)
        for i, u in enumerate(units):
            lanes = slice(i * lev, (i + 1) * lev)
            one = x_ref[b, pl.ds(u * pad, cols)]
            two = x_ref[b + quarter, pl.ds(u * pad, cols)]
            S[at, lanes] = one + two
            D[at, lanes] = one - two
    tall = size // 128
    first = 0
    for row, members in groups:
        lanes = slice(first * lev, (first + len(members)) * lev)
        first += len(members)

        def matrix(ref, e, row=row):
            starts = [(tall - 1 - b) * 128 for b in range(tall)]
            return jnp.concatenate([ref[row, e, :, st : st + size] for st in starts], axis=0)

        for e, (src, dst) in enumerate(((S, Y), (D, Z))):
            x = src[:, lanes]
            xh = x.astype(bf16)
            xl = (x - xh.astype(f32)).astype(bf16)
            mh = matrix(hi_ref, e)
            ml = matrix(lo_ref, e)
            if len(members) == 1:
                both = jnp.dot(mh, jnp.concatenate([xh, xl], axis=1), preferred_element_type=f32)
                small = jnp.dot(ml, xh, preferred_element_type=f32)
                dst[:, lanes] = both[:, :lev] + (both[:, lev:] + small)
            else:
                left = jnp.concatenate([mh, mh, ml], axis=1)
                right = jnp.concatenate([xh, xl, xh], axis=0)
                dst[:, lanes] = jnp.dot(left, right, preferred_element_type=f32)
    for b in range(quarter):
        at = slice(b * cols, (b + 1) * cols)
        for i, u in enumerate(units):
            lanes = slice(i * lev, (i + 1) * lev)
            y = Y[at, lanes]
            z = Z[at, lanes]
            y_ref[b, pl.ds(u * pad, cols)] = y + z
            y_ref[b + quarter, pl.ds(u * pad, cols)] = y - z


def filtered(groups, hi, lo, whole, after, cols):
    _, tall, lev = whole.shape
    count = sum(len(members) for _, members in groups)
    work = pltpu.VMEM((hi.shape[-1] - 128 * 5, count * lev), f32)
    return pl.pallas_call(
        functools.partial(filter_kernel, groups, cols),
        in_specs=[vmem()] * 3 + [any_space()],
        out_specs=vmem(),
        out_shape=jax.ShapeDtypeStruct(whole.shape, f32),
        scratch_shapes=[work] * 4,
        compiler_params=params(28),
    )(hi, lo, whole, after)


def join_kernel(cols, rows, ids_ref, y_ref, u_ref, v_ref, _, out_ref, held, moved, result, sem, out_sem):
    @pl.when(ids_ref[3] != 0)
    def _():
        pad = padded(cols)
        copies = [pltpu.make_async_copy(y_ref.at[:, pl.ds(u * pad, pad)], held.at[u], sem.at[u]) for u in range(4)]
        copies += [pltpu.make_async_copy(ref, moved.at[u], sem.at[4 + u]) for u, ref in enumerate((u_ref, v_ref))]
        outs = [pltpu.make_async_copy(result.at[c], out_ref.at[c], out_sem.at[c]) for c in range(3)]
        for copy in copies:
            copy.start()
        for c, inner, wait in ((0, moved.at[0], 4), (1, moved.at[1], 5), (2, held.at[3], 3)):
            copies[c].wait()
            copies[wait].wait()
            for d in range(GROUP):
                result[c, pl.ds(EDGE[d], cols, stride=rows), :] = held[c, d, 0:cols]
                result[c, pl.ds(INNER[d], cols, stride=rows), :] = inner[d, 0:cols]
            outs[c].start()
        for c in range(3):
            outs[c].wait()


def joined(ids, whole, moved_u, moved_v, other, cols, rows):
    lev = whole.shape[-1]
    pad = padded(cols)
    return pl.pallas_call(
        functools.partial(join_kernel, cols, rows),
        in_specs=[smem()] + [any_space()] * 4,
        out_specs=any_space(),
        out_shape=jax.ShapeDtypeStruct(other.shape, f32),
        scratch_shapes=[
            pltpu.VMEM((4, GROUP, pad, lev), f32),
            pltpu.VMEM((2, GROUP, pad, lev), f32),
            pltpu.VMEM(other.shape, f32),
            pltpu.SemaphoreType.DMA((6,)),
            pltpu.SemaphoreType.DMA((3,)),
        ],
        input_output_aliases={4: 0},
        compiler_params=params(16),
    )(ids, whole, moved_u, moved_v, other)


def tie_kernel(x_ref, _, out_ref):
    pass


def tied(x, y):
    return pl.pallas_call(
        tie_kernel,
        in_specs=[any_space()] * 2,
        out_specs=any_space(),
        out_shape=jax.ShapeDtypeStruct(x.shape, x.dtype),
        input_output_aliases={0: 0},
        compiler_params=params(1),
    )(x, y)


def hollow_kernel(out_ref):
    pass


def hollow(x):
    return pl.pallas_call(
        hollow_kernel,
        out_specs=any_space(),
        out_shape=jax.ShapeDtypeStruct(x.shape, x.dtype),
        compiler_params=params(1),
    )()


def swapped(x):
    return lax.all_to_all(x, "lon", split_axis=0, concat_axis=0, tiled=True)


def body(state, cutoffs):
    lat_count = lax.axis_size("lat")
    lon_count = lax.axis_size("lon")
    _, cols, rows, lev = state.shape
    total_lat = rows * lat_count
    total_lon = cols * lon_count
    band = lax.axis_index("lat")
    me = lax.axis_index("lon")
    quarter = lat_count // 4
    polar = (band < quarter) | (band >= lat_count - quarter)
    ids = jnp.stack([me, band, lat_count - 1 - band, polar.astype(jnp.int32)]).astype(jnp.int32)

    up = [(i, i + 1) for i in range(lat_count - 1)]
    down = [(j, i) for i, j in up]
    right = [(i, (i + 1) % lon_count) for i in range(lon_count)]
    left = [(j, i) for i, j in right]

    flat = state.reshape(3, cols * rows, lev)
    last = state[:, cols - HALO :].reshape(3, HALO * rows, lev)
    first = state[:, :HALO].reshape(3, HALO * rows, lev)
    west = lax.ppermute(last, "lon", right)
    east_ = lax.ppermute(first, "lon", left)
    outward = [(b, b + quarter) for b in range(quarter)]
    outward += [(b, b - quarter) for b in range(lat_count - quarter, lat_count)]
    inward = [(j, i) for i, j in outward]
    near = band * rows - HALO + jnp.arange(rows + 2 * HALO, dtype=jnp.int32)
    latitude = (-90.0 + (near.astype(f32) + 0.5) * (180.0 / total_lat)) * (jnp.pi / 180.0)
    metric = 1.0 / jnp.maximum(jnp.cos(latitude), 1.0 / CAP)

    planes, own_north, own_south = split_planes(flat, (last, first), cols, rows)
    send_north, send_south = with_columns(west, east_, own_north, own_south, cols, rows)
    wanted = jnp.stack([edge_row(me), inner_row(me)])
    chosen = wanted[:, None] == jnp.arange(rows, dtype=jnp.int32)[None, :]
    picked = jnp.sum(jnp.where(chosen, cutoffs.astype(f32)[None, :], 0.0), axis=1)
    picked = tied(picked, send_north)
    offsets = offset_values(picked, total_lon)
    token = jnp.zeros((8, lev), f32)
    packed = offsets[1].reshape(GROUP * PACK, lev)
    hi, lo = skewed(offsets, token)
    halo_north = lax.ppermute(send_south, "lat", up)
    halo_south = lax.ppermute(send_north, "lat", down)

    u, v, theta, rim, raw = inner_rows(metric, planes, west, east_, packed, send_north, cols, rows)
    moved_u = lax.ppermute(u, "lat", outward)
    moved_v = lax.ppermute(v, "lat", outward)
    def edges(near_pole, after):
        inner = (u, v, theta)
        return edge_rows(near_pole, ids, metric, raw, rim, halo_north, halo_south, inner, after, cols, rows)

    pieces = edges(True, lo)

    def elsewhere(x, first, after):
        hi, lo = unpacked(first, total_lon, after)
        return swapped(filtered(((0, (0,)),), hi, lo, swapped(x), after, cols))

    def idle(x, *_):
        return hollow(x)

    def near_pole(x, after):
        return swapped(filtered(((0, (0, 1)), (0, (2,)), (1, (3,))), hi, lo, x, after, cols))

    def same(x, *_):
        return x

    whole = lax.cond(polar, swapped, same, pieces)
    back_u = lax.cond(polar, idle, elsewhere, moved_u, moved_u, tied(token, whole))
    moved_back_u = lax.ppermute(back_u, "lat", inward)
    back_v = lax.cond(polar, idle, elsewhere, moved_v, moved_u, tied(token, whole))
    moved_back_v = lax.ppermute(back_v, "lat", inward)
    other = edges(False, tied(token, back_v))
    pieces = lax.cond(polar, near_pole, same, whole, tied(token, back_v))
    return joined(ids, pieces, moved_back_u, moved_back_v, other, cols, rows).reshape(3, cols, rows, lev)


def solution(mesh):
    placed = (P(None, "lon", "lat", None), P("lat"))
    return jax.shard_map(
        body, mesh=mesh, in_specs=placed, out_specs=P(None, "lon", "lat", None), check_vma=False
    )
```

```python
import functools

import jax
import jax.numpy as jnp
import numpy as np
from jax import lax
from jax.experimental import pallas as pl
from jax.experimental.pallas import tpu as pltpu
from jax.sharding import PartitionSpec as P

SUBSTEPS = 2
HALO = 1 + 2 * SUBSTEPS
ADV = 0.5
SOUND = 0.8
CAP = 2.0
LEAD = 16
GROUP = 8
UNROLL = 4
PACK = 3
MIB = 1024 * 1024

f32 = jnp.float32
bf16 = jnp.bfloat16


def params(mib):
    return pltpu.CompilerParams(vmem_limit_bytes=mib * MIB)


def vmem():
    return pl.BlockSpec(memory_space=pltpu.VMEM)


def smem():
    return pl.BlockSpec(memory_space=pltpu.SMEM)


def edge_row(d):
    return jnp.where(d < 4, d, d + 8)


def inner_row(d):
    return d + 4


EDGE = [d if d < 4 else d + 8 for d in range(GROUP)]
INNER = [d + 4 for d in range(GROUP)]


def padded(cols):
    return -(-cols // 8) * 8


def window(cols):
    return -(-(8 + cols + HALO) // 8) * 8


def cost(micros):
    return pl.CostEstimate(flops=0, bytes_accessed=int(micros * 3.69e6), transcendentals=0)


def any_space():
    return pl.BlockSpec(memory_space=pltpu.MemorySpace.HBM)


def split_kernel(cols, rows, x_ref, _, __, planes_ref, north_ref, south_ref, hold, P, sem, out_sem):
    count = HALO - 1
    loads = [pltpu.make_async_copy(x_ref.at[c], hold.at[c], sem.at[c]) for c in range(3)]
    for copy in loads:
        copy.start()
    outs = []
    for c in range(3):
        loads[c].wait()
        for r in range(rows):
            P[c, r, pl.ds(8, cols)] = hold[c, pl.ds(r, cols, stride=rows), :]
        mine = [
            (P.at[c, pl.ds(0, count)], north_ref.at[pl.ds(count * c, count)]),
            (P.at[c, pl.ds(rows - count, count)], south_ref.at[pl.ds(count * c, count)]),
            (P.at[c], planes_ref.at[c]),
        ]
        if c == 2:
            mine.append((P.at[c, pl.ds(count, 1)], north_ref.at[pl.ds(3 * count, 1)]))
            mine.append((P.at[c, pl.ds(rows - HALO, 1)], south_ref.at[pl.ds(3 * count, 1)]))
        for s, d in mine:
            outs.append(pltpu.make_async_copy(s, d, out_sem.at[len(outs)]))
            outs[-1].start()
    for copy in outs:
        copy.wait()


def split_planes(flat, after, cols, rows):
    lev = flat.shape[-1]
    wide = window(cols)
    edge = jax.ShapeDtypeStruct((3 * (HALO - 1) + 1, wide, lev), f32)
    planes = (3, rows, wide, lev)
    return pl.pallas_call(
        functools.partial(split_kernel, cols, rows),
        in_specs=[any_space()] * 3,
        out_specs=[any_space()] * 3,
        out_shape=[jax.ShapeDtypeStruct(planes, f32), edge, edge],
        scratch_shapes=[
            pltpu.VMEM(flat.shape, f32),
            pltpu.VMEM(planes, f32),
            pltpu.SemaphoreType.DMA((3,)),
            pltpu.SemaphoreType.DMA((11,)),
        ],
        compiler_params=params(60),
    )(flat, *after)


def column_kernel(cols, rows, west_ref, east_ref, _, __, north_ref, south_ref, W, E, sem, out_sem):
    at = (8 + cols) // 8 * 8
    off = 8 + cols - at
    ends = ((north_ref, 0), (south_ref, 1))
    loads = [pltpu.make_async_copy(ref.at[:, pl.ds(at, 16)], E.at[k], sem.at[k]) for ref, k in ends]
    for copy in loads:
        copy.start()
    for k, (base, last) in enumerate(((0, HALO - 1), (rows - HALO + 1, rows - HALO))):
        planes = [(c, base + j) for c in range(3) for j in range(HALO - 1)] + [(2, last)]
        for n, (c, r) in enumerate(planes):
            W[k, n, pl.ds(8 - HALO, HALO)] = west_ref[c, pl.ds(r, HALO, stride=rows), :]
        loads[k].wait()
        for n, (c, r) in enumerate(planes):
            E[k, n, pl.ds(off, HALO)] = east_ref[c, pl.ds(r, HALO, stride=rows), :]
    outs = [pltpu.make_async_copy(E.at[k], ref.at[:, pl.ds(at, 16)], sem.at[k]) for ref, k in ends]
    outs += [pltpu.make_async_copy(W.at[k], ref.at[:, pl.ds(0, 8)], out_sem.at[k]) for ref, k in ends]
    for copy in outs:
        copy.start()
    for copy in outs:
        copy.wait()


def with_columns(west, east_, north, south, cols, rows):
    count, _, lev = north.shape
    return pl.pallas_call(
        functools.partial(column_kernel, cols, rows),
        in_specs=[vmem(), vmem(), any_space(), any_space()],
        out_specs=[any_space()] * 2,
        out_shape=[jax.ShapeDtypeStruct(north.shape, f32)] * 2,
        scratch_shapes=[
            pltpu.VMEM((2, count, 8, lev), f32),
            pltpu.VMEM((2, count, 16, lev), f32),
            pltpu.SemaphoreType.DMA((2,)),
            pltpu.SemaphoreType.DMA((2,)),
        ],
        input_output_aliases={2: 0, 3: 1},
        compiler_params=params(4),
    )(west, east_, north, south)


def east(W, r):
    cols = W.shape[1] - 16
    return W[r, pl.ds(9, cols)] - W[r, pl.ds(7, cols)]


def stage_steps(metric_ref, base, U, V, T, A, B, C, keep):
    mid = pl.ds(8, U.shape[1] - 16)

    def metric(i):
        return metric_ref[i + (HALO - base)]

    def advect(i, fields=None):
        mu = metric(i) * (0.5 * ADV) * U[i, mid]
        nv = (0.5 * ADV) * V[i, mid]
        for W, out in fields or ((U, A), (V, B), (T, C)):
            out[i, mid] = W[i, mid] - (mu * east(W, i) + nv * (W[i + 1, mid] - W[i - 1, mid]))

    def advect_theta(i):
        advect(i, ((T, C),))

    def wind_u(i):
        A[i, mid] = A[i, mid] - (metric(i) * (0.5 * SOUND)) * east(C, i)

    def wind_v(i):
        B[i, mid] = keep(i, B[i, mid] - (0.5 * SOUND) * (C[i + 1, mid] - C[i - 1, mid]))

    def theta(i):
        m = metric(i) * (0.5 * SOUND)
        C[i, mid] = keep(i, C[i, mid] - (m * east(A, i) + (0.5 * SOUND) * (B[i + 1, mid] - B[i - 1, mid])))

    return advect, advect_theta, wind_u, wind_v, theta


def sweep(fn, *spans):
    for lo, hi in spans:

        def step(i, carry):
            fn(i)
            return carry

        lax.fori_loop(lo, hi, step, 0, unroll=UNROLL)


def inner_kernel(
    cols, rows, metric_ref, planes_ref, west_ref, east_ref, off_ref, _, u_ref, v_ref, theta_ref, rim_ref, raw_ref, *scratch
):
    U, V, T, A, B, C, sem, out_sem = scratch
    own = slice(LEAD, LEAD + cols)
    wide = pl.ds(LEAD - 8, window(cols))
    loads = [pltpu.make_async_copy(planes_ref.at[c], W.at[:, wide], sem.at[c]) for c, W in enumerate((U, V, T))]
    for copy in loads:
        copy.start()
    outs = []
    for c, W in enumerate((U, V, T)):
        loads[c].wait()

        for r in range(rows):
            W[r, pl.ds(LEAD - HALO, HALO)] = west_ref[c, pl.ds(r, HALO, stride=rows), :]
            W[r, pl.ds(LEAD + cols, HALO)] = east_ref[c, pl.ds(r, HALO, stride=rows), :]
        for k, at in ((0, 0), (1, rows - 2)):
            outs.append((W.at[pl.ds(at, 2), wide], raw_ref.at[c, pl.ds(2 * k, 2)]))
    advect, _, wind_u, wind_v, theta = stage_steps(metric_ref, 0, U, V, T, A, B, C, lambda r, x: x)
    sweep(advect, (1, rows - 1))
    sweep(wind_u, (1, rows - 1))
    sweep(wind_v, (2, rows - 2))
    sweep(theta, (3, rows - 3))
    sweep(wind_u, (3, rows - 3))
    sweep(wind_v, (4, rows - 4))
    sweep(theta, (5, rows - 5))
    for c, W in enumerate((A, B, C)):
        for k, at in ((0, 1), (1, rows - 6)):
            outs.append((W.at[pl.ds(at, 5), wide], rim_ref.at[c, pl.ds(5 * k, 5)]))
    outs = [pltpu.make_async_copy(a, b, out_sem.at[i]) for i, (a, b) in enumerate(outs)]
    for copy in outs:
        copy.start()
    pad = padded(cols)
    for d in range(GROUP):
        u_ref[d, pl.ds(0, cols)] = A[INNER[d], own]
        u_ref[d, pl.ds(cols, PACK)] = off_ref[PACK * d : PACK * (d + 1)]
        v_ref[d, pl.ds(0, cols)] = B[INNER[d], own]
        theta_ref[d, pl.ds(0, cols)] = C[INNER[d], own]
    for copy in outs:
        copy.wait()


def inner_rows(metric, planes, west, east_, offsets, after, cols, rows):
    lev = planes.shape[-1]
    pad = padded(cols)
    wide = window(cols)
    shapes = [(GROUP, pad, lev)] * 3 + [(3, 10, wide, lev), (3, 4, wide, lev)]
    return pl.pallas_call(
        functools.partial(inner_kernel, cols, rows),
        in_specs=[smem(), any_space(), vmem(), vmem(), vmem(), any_space()],
        out_specs=[vmem()] * 3 + [any_space()] * 2,
        out_shape=[jax.ShapeDtypeStruct(s, f32) for s in shapes],
        scratch_shapes=[pltpu.VMEM((rows, LEAD + wide, lev), f32)] * 6
        + [pltpu.SemaphoreType.DMA((3,)), pltpu.SemaphoreType.DMA((12,))],
        compiler_params=params(60),
        cost_estimate=cost(9),
    )(metric, planes, west, east_, offsets, after)


def edge_kernel(cols, rows, near_pole, ids_ref, *refs):
    @pl.when((ids_ref[3] != 0) if near_pole else (ids_ref[3] == 0))
    def _():
        edge_steps(cols, rows, near_pole, ids_ref, *refs)


def edge_steps(
    cols, rows, near_pole, ids_ref, metric_ref, raw_ref, rim_ref, hn_ref, hs_ref, u_ref, v_ref, theta_ref, _, out_ref, *scratch
):
    U, V, T, A, B, C, sem, move_sem, *more = scratch
    own = slice(LEAD, LEAD + cols)
    wide = pl.ds(LEAD - 8, window(cols))
    pad = padded(cols)
    count = HALO - 1
    loads = []
    for c, W in enumerate((U, V, T)):
        loads.append((hn_ref.at[pl.ds(count * c, count)], W.at[pl.ds(1, count), wide]))
        loads.append((hs_ref.at[pl.ds(count * c, count)], W.at[pl.ds(HALO + rows, count), wide]))
        loads.append((raw_ref.at[c, pl.ds(0, 2)], W.at[pl.ds(HALO, 2), wide]))
        loads.append((raw_ref.at[c, pl.ds(2, 2)], W.at[pl.ds(HALO + rows - 2, 2), wide]))
    loads.append((hn_ref.at[pl.ds(3 * count, 1)], T.at[pl.ds(0, 1), wide]))
    loads.append((hs_ref.at[pl.ds(3 * count, 1)], T.at[pl.ds(2 * HALO + rows - 1, 1), wide]))
    for c, W in enumerate((A, B, C)):
        loads.append((rim_ref.at[c, pl.ds(0, 5)], W.at[pl.ds(HALO + 1, 5), wide]))
        loads.append((rim_ref.at[c, pl.ds(5, 5)], W.at[pl.ds(HALO + rows - 6, 5), wide]))
    loads = [pltpu.make_async_copy(a, b, sem.at[i]) for i, (a, b) in enumerate(loads)]
    for copy in loads:
        copy.start()
    for copy in loads[:14]:
        copy.wait()
    has_north = jnp.where(ids_ref[1] > 0, 1.0, 0.0)
    has_south = jnp.where(ids_ref[2] > 0, 1.0, 0.0)

    def keep(i, x):
        return x * jnp.where(i >= HALO + rows, has_south, jnp.where(i < HALO, has_north, 1.0))

    advect, advect_theta, wind_u, wind_v, theta = stage_steps(metric_ref, HALO, U, V, T, A, B, C, keep)

    def ends(fn, lo, hi):
        sweep(fn, (HALO + lo, HALO + hi), (HALO + rows - hi, HALO + rows - lo))

    ends(advect, -3, 1)
    ends(advect_theta, -4, -3)
    for copy in loads[14:]:
        copy.wait()
    ends(wind_u, -2, 1)
    ends(wind_v, -3, 2)
    ends(theta, -2, 3)
    ends(wind_u, 0, 3)
    ends(wind_v, -1, 4)
    ends(theta, 0, 5)

    if near_pole:
        inside = pltpu.make_async_copy(
            theta_ref.at[pl.ds(1, GROUP - 2)], out_ref.at[pl.ds(1, GROUP - 2), pl.ds(3 * pad, pad)], move_sem.at[0]
        )
        inside.start()
        for d in range(GROUP):
            for c, W in enumerate((A, B, C)):
                out_ref[d, pl.ds(c * pad, cols)] = W[EDGE[d] + HALO, own]
        for d in (0, GROUP - 1):
            out_ref[d, pl.ds(3 * pad, cols)] = C[INNER[d] + HALO, own]
        inside.wait()
    else:
        hold, moved, out_sem = more
        inside = [
            pltpu.make_async_copy(ref, moved.at[:, pl.ds(c * pad, pad)], move_sem.at[c])
            for c, ref in enumerate((u_ref, v_ref, theta_ref))
        ]
        for copy in inside:
            copy.start()
        for copy in inside:
            copy.wait()
        outs = [pltpu.make_async_copy(hold.at[c], out_ref.at[c], out_sem.at[c]) for c in range(3)]
        for c, W in enumerate((A, B, C)):
            for d in range(GROUP):
                hold[c, pl.ds(EDGE[d], cols, stride=rows), :] = W[EDGE[d] + HALO, own]
                if c == 2 and d in (0, GROUP - 1):
                    value = C[INNER[d] + HALO, own]
                else:
                    value = moved[d, pl.ds(c * pad, cols)]
                hold[c, pl.ds(INNER[d], cols, stride=rows), :] = value
            outs[c].start()
        for out in outs:
            out.wait()


def edge_rows(near_pole, ids, metric, raw, rim, hn, hs, inner, after, cols, rows):
    lev = raw.shape[-1]
    pad = padded(cols)
    whole = (3, cols * rows, lev)
    scratch = [pltpu.VMEM((rows + 2 * HALO, LEAD + window(cols), lev), f32)] * 6
    scratch += [pltpu.SemaphoreType.DMA((20,)), pltpu.SemaphoreType.DMA((3,))]
    if not near_pole:
        scratch += [pltpu.VMEM(whole, f32), pltpu.VMEM((GROUP, 3 * pad, lev), f32), pltpu.SemaphoreType.DMA((3,))]
    return pl.pallas_call(
        functools.partial(edge_kernel, cols, rows, near_pole),
        in_specs=[smem(), smem()] + [any_space()] * 8,
        out_specs=vmem() if near_pole else any_space(),
        out_shape=jax.ShapeDtypeStruct((GROUP, 4 * pad, lev) if near_pole else whole, f32),
        scratch_shapes=scratch,
        compiler_params=params(57 if near_pole else 60),
    )(ids, metric, raw, rim, hn, hs, *inner, after)


def offset_tables(length):
    half = length // 2
    pad = -(-half // 256) * 256
    n = np.arange(2 * pad) - pad
    tables = []
    for first in (0, 1):
        wave = np.arange(first, half + 1, 2)
        weight = np.where((wave == 0) | (wave == half), 1.0, 2.0) / length
        angle = (wave[:, None] * n[None, :]) % length * (2.0 * np.pi / length)
        tables.append((wave, (np.cos(angle) * weight[:, None]).astype(np.float32)))
    return tables


def offset_values(limits, length):
    values = []
    for wave, table in offset_tables(length):
        w = jnp.asarray(wave, f32)
        lim = limits[:, None]
        factor = jnp.where(w[None, :] <= lim, 1.0, (lim / jnp.maximum(w, 1.0)[None, :]) ** 2)
        values.append(jnp.dot(factor, jnp.asarray(table), precision=lax.Precision.HIGHEST, preferred_element_type=f32))
    return jnp.stack(values, axis=1)[:, :, None, :]


def skew(p, store):
    width = p.shape[-1]
    line = lax.broadcasted_iota(jnp.int32, (8, width), 0)
    x = jnp.broadcast_to(p, (8, width))
    for bit in range(3):
        x = jnp.where((line & (1 << bit)) != 0, pltpu.roll(x, 1 << bit, 1), x)
    for pair in range(8):
        two = [pltpu.roll(x, 8 * g, 1)[:, 128:] if g else x[:, 128:] for g in (2 * pair, 2 * pair + 1)]
        y = jnp.concatenate(two, axis=0)
        hi = y.astype(bf16)
        store(16 * pair, hi, (y - hi.astype(f32)).astype(bf16))


def unpack_kernel(length, x_ref, _, hi_ref, lo_ref):
    cols = length // GROUP
    lines = [x_ref[d, cols + j : cols + j + 1] for d in range(GROUP) for j in range(PACK)]
    half = len(lines) // 2
    for e in range(2):

        def store(at, hi, lo, e=e):
            hi_ref[0, e, at : at + 16] = hi
            lo_ref[0, e, at : at + 16] = lo

        skew(jnp.concatenate(lines[e * half : (e + 1) * half], axis=1), store)


def unpacked(x, length, after):
    width = GROUP * PACK * x.shape[-1] // 2
    out = jax.ShapeDtypeStruct((1, 2, 128, width - 128), bf16)
    return pl.pallas_call(
        functools.partial(unpack_kernel, length),
        in_specs=[vmem(), any_space()],
        out_specs=[vmem()] * 2,
        out_shape=[out, out],
        compiler_params=params(16),
    )(x, after)


def skew_kernel(p_ref, _, hi_ref, lo_ref):
    rows, parts, _, width = p_ref.shape
    for r in range(rows):
        for e in range(parts):

            def store(at, hi, lo, r=r, e=e):
                hi_ref[r, e, at : at + 16] = hi
                lo_ref[r, e, at : at + 16] = lo

            skew(p_ref[r, e], store)


def skewed(values, after):
    rows, parts, _, width = values.shape
    out = jax.ShapeDtypeStruct((rows, parts, 128, width - 128), bf16)
    return pl.pallas_call(
        skew_kernel,
        in_specs=[vmem(), any_space()],
        out_specs=[vmem()] * 2,
        out_shape=[out, out],
        compiler_params=params(16),
    )(values, after)


def filter_kernel(groups, cols, hi_ref, lo_ref, x_ref, _, y_ref, S, D, Y, Z):
    quarter = GROUP // 2
    size = S.shape[0]
    lev = x_ref.shape[-1]
    pad = padded(cols)
    units = [u for _, members in groups for u in members]
    S[quarter * cols :] = jnp.zeros((size - quarter * cols, S.shape[1]), f32)
    D[quarter * cols :] = jnp.zeros((size - quarter * cols, S.shape[1]), f32)
    for b in range(quarter):
        at = slice(b * cols, (b + 1) * cols)
        for i, u in enumerate(units):
            lanes = slice(i * lev, (i + 1) * lev)
            one = x_ref[b, pl.ds(u * pad, cols)]
            two = x_ref[b + quarter, pl.ds(u * pad, cols)]
            S[at, lanes] = one + two
            D[at, lanes] = one - two
    tall = size // 128
    first = 0
    for row, members in groups:
        lanes = slice(first * lev, (first + len(members)) * lev)
        first += len(members)

        def matrix(ref, e, row=row):
            starts = [(tall - 1 - b) * 128 for b in range(tall)]
            return jnp.concatenate([ref[row, e, :, st : st + size] for st in starts], axis=0)

        for e, (src, dst) in enumerate(((S, Y), (D, Z))):
            x = src[:, lanes]
            xh = x.astype(bf16)
            xl = (x - xh.astype(f32)).astype(bf16)
            mh = matrix(hi_ref, e)
            ml = matrix(lo_ref, e)
            if len(members) == 1:
                both = jnp.dot(mh, jnp.concatenate([xh, xl], axis=1), preferred_element_type=f32)
                small = jnp.dot(ml, xh, preferred_element_type=f32)
                dst[:, lanes] = both[:, :lev] + (both[:, lev:] + small)
            else:
                left = jnp.concatenate([mh, mh, ml], axis=1)
                right = jnp.concatenate([xh, xl, xh], axis=0)
                dst[:, lanes] = jnp.dot(left, right, preferred_element_type=f32)
    for b in range(quarter):
        at = slice(b * cols, (b + 1) * cols)
        for i, u in enumerate(units):
            lanes = slice(i * lev, (i + 1) * lev)
            y = Y[at, lanes]
            z = Z[at, lanes]
            y_ref[b, pl.ds(u * pad, cols)] = y + z
            y_ref[b + quarter, pl.ds(u * pad, cols)] = y - z


def filtered(groups, hi, lo, whole, after, cols):
    _, tall, lev = whole.shape
    count = sum(len(members) for _, members in groups)
    work = pltpu.VMEM((hi.shape[-1] - 128 * 5, count * lev), f32)
    return pl.pallas_call(
        functools.partial(filter_kernel, groups, cols),
        in_specs=[vmem()] * 3 + [any_space()],
        out_specs=vmem(),
        out_shape=jax.ShapeDtypeStruct(whole.shape, f32),
        scratch_shapes=[work] * 4,
        compiler_params=params(28),
    )(hi, lo, whole, after)


def join_kernel(cols, rows, ids_ref, y_ref, u_ref, v_ref, _, out_ref, held, moved, result, sem, out_sem):
    @pl.when(ids_ref[3] != 0)
    def _():
        pad = padded(cols)
        copies = [pltpu.make_async_copy(y_ref.at[:, pl.ds(u * pad, pad)], held.at[u], sem.at[u]) for u in range(4)]
        copies += [pltpu.make_async_copy(ref, moved.at[u], sem.at[4 + u]) for u, ref in enumerate((u_ref, v_ref))]
        outs = [pltpu.make_async_copy(result.at[c], out_ref.at[c], out_sem.at[c]) for c in range(3)]
        for copy in copies:
            copy.start()
        for c, inner, wait in ((0, moved.at[0], 4), (1, moved.at[1], 5), (2, held.at[3], 3)):
            copies[c].wait()
            copies[wait].wait()
            for d in range(GROUP):
                result[c, pl.ds(EDGE[d], cols, stride=rows), :] = held[c, d, 0:cols]
                result[c, pl.ds(INNER[d], cols, stride=rows), :] = inner[d, 0:cols]
            outs[c].start()
        for c in range(3):
            outs[c].wait()


def joined(ids, whole, moved_u, moved_v, other, cols, rows):
    lev = whole.shape[-1]
    pad = padded(cols)
    return pl.pallas_call(
        functools.partial(join_kernel, cols, rows),
        in_specs=[smem()] + [any_space()] * 4,
        out_specs=any_space(),
        out_shape=jax.ShapeDtypeStruct(other.shape, f32),
        scratch_shapes=[
            pltpu.VMEM((4, GROUP, pad, lev), f32),
            pltpu.VMEM((2, GROUP, pad, lev), f32),
            pltpu.VMEM(other.shape, f32),
            pltpu.SemaphoreType.DMA((6,)),
            pltpu.SemaphoreType.DMA((3,)),
        ],
        input_output_aliases={4: 0},
        compiler_params=params(16),
    )(ids, whole, moved_u, moved_v, other)


def tie_kernel(x_ref, _, out_ref):
    pass


def tied(x, y):
    return pl.pallas_call(
        tie_kernel,
        in_specs=[any_space()] * 2,
        out_specs=any_space(),
        out_shape=jax.ShapeDtypeStruct(x.shape, x.dtype),
        input_output_aliases={0: 0},
        compiler_params=params(1),
    )(x, y)


def hollow_kernel(out_ref):
    pass


def hollow(x):
    return pl.pallas_call(
        hollow_kernel,
        out_specs=any_space(),
        out_shape=jax.ShapeDtypeStruct(x.shape, x.dtype),
        compiler_params=params(1),
    )()


def swapped(x):
    return lax.all_to_all(x, "lon", split_axis=0, concat_axis=0, tiled=True)


def body(state, cutoffs):
    lat_count = lax.axis_size("lat")
    lon_count = lax.axis_size("lon")
    _, cols, rows, lev = state.shape
    total_lat = rows * lat_count
    total_lon = cols * lon_count
    band = lax.axis_index("lat")
    me = lax.axis_index("lon")
    quarter = lat_count // 4
    polar = (band < quarter) | (band >= lat_count - quarter)
    ids = jnp.stack([me, band, lat_count - 1 - band, polar.astype(jnp.int32)]).astype(jnp.int32)

    up = [(i, i + 1) for i in range(lat_count - 1)]
    down = [(j, i) for i, j in up]
    right = [(i, (i + 1) % lon_count) for i in range(lon_count)]
    left = [(j, i) for i, j in right]

    flat = state.reshape(3, cols * rows, lev)
    last = state[:, cols - HALO :].reshape(3, HALO * rows, lev)
    first = state[:, :HALO].reshape(3, HALO * rows, lev)
    west = lax.ppermute(last, "lon", right)
    east_ = lax.ppermute(first, "lon", left)
    outward = [(b, b + quarter) for b in range(quarter)]
    outward += [(b, b - quarter) for b in range(lat_count - quarter, lat_count)]
    inward = [(j, i) for i, j in outward]
    near = band * rows - HALO + jnp.arange(rows + 2 * HALO, dtype=jnp.int32)
    latitude = (-90.0 + (near.astype(f32) + 0.5) * (180.0 / total_lat)) * (jnp.pi / 180.0)
    metric = 1.0 / jnp.maximum(jnp.cos(latitude), 1.0 / CAP)

    planes, own_north, own_south = split_planes(flat, (last, first), cols, rows)
    send_north, send_south = with_columns(west, east_, own_north, own_south, cols, rows)
    wanted = jnp.stack([edge_row(me), inner_row(me)])
    chosen = wanted[:, None] == jnp.arange(rows, dtype=jnp.int32)[None, :]
    picked = jnp.sum(jnp.where(chosen, cutoffs.astype(f32)[None, :], 0.0), axis=1)
    picked = tied(picked, send_north)
    offsets = offset_values(picked, total_lon)
    token = jnp.zeros((8, lev), f32)
    packed = offsets[1].reshape(GROUP * PACK, lev)
    hi, lo = skewed(offsets, token)
    halo_north = lax.ppermute(send_south, "lat", up)
    halo_south = lax.ppermute(send_north, "lat", down)

    u, v, theta, rim, raw = inner_rows(metric, planes, west, east_, packed, send_north, cols, rows)
    moved_u = lax.ppermute(u, "lat", outward)
    moved_v = lax.ppermute(v, "lat", outward)
    def edges(near_pole, after):
        inner = (u, v, theta)
        return edge_rows(near_pole, ids, metric, raw, rim, halo_north, halo_south, inner, after, cols, rows)

    def elsewhere(x, first, after):
        hi, lo = unpacked(first, total_lon, after)
        return swapped(filtered(((0, (0,)),), hi, lo, swapped(x), after, cols))

    def idle(x, *_):
        return hollow(x)

    def near_pole(x, after):
        return swapped(filtered(((0, (0, 1)), (0, (2,)), (1, (3,))), hi, lo, x, after, cols))

    def same(x, *_):
        return x

    def first_half(after):
        return swapped(edges(True, after))

    blank = jax.ShapeDtypeStruct((GROUP, 4 * padded(cols), lev), f32)
    whole = lax.cond(polar, first_half, lambda _: hollow(blank), lo)
    back_u = lax.cond(polar, idle, elsewhere, moved_u, moved_u, tied(token, whole))
    moved_back_u = lax.ppermute(back_u, "lat", inward)
    back_v = lax.cond(polar, idle, elsewhere, moved_v, moved_u, tied(token, whole))
    moved_back_v = lax.ppermute(back_v, "lat", inward)
    other = lax.cond(polar, lambda _: hollow(flat), lambda after: edges(False, after), tied(token, back_v))
    pieces = lax.cond(polar, near_pole, same, whole, tied(token, back_v))
    return joined(ids, pieces, moved_back_u, moved_back_v, other, cols, rows).reshape(3, cols, rows, lev)


def solution(mesh):
    placed = (P(None, "lon", "lat", None), P("lat"))
    return jax.shard_map(
        body, mesh=mesh, in_specs=placed, out_specs=P(None, "lon", "lat", None), check_vma=False
    )
```

```python
import functools

import jax
import jax.numpy as jnp
import numpy as np
from jax import lax
from jax.experimental import pallas as pl
from jax.experimental.pallas import tpu as pltpu
from jax.sharding import PartitionSpec as P

SUBSTEPS = 2
HALO = 1 + 2 * SUBSTEPS
ADV = 0.5
SOUND = 0.8
CAP = 2.0
LEAD = 16
GROUP = 8
UNROLL = 4
PACK = 3
MIB = 1024 * 1024

f32 = jnp.float32
bf16 = jnp.bfloat16


def params(mib):
    return pltpu.CompilerParams(vmem_limit_bytes=mib * MIB)


def vmem():
    return pl.BlockSpec(memory_space=pltpu.VMEM)


def smem():
    return pl.BlockSpec(memory_space=pltpu.SMEM)


def edge_row(d):
    return jnp.where(d < 4, d, d + 8)


def inner_row(d):
    return d + 4


EDGE = [d if d < 4 else d + 8 for d in range(GROUP)]
INNER = [d + 4 for d in range(GROUP)]


def padded(cols):
    return -(-cols // 8) * 8


def window(cols):
    return -(-(8 + cols + HALO) // 8) * 8


def cost(micros):
    return pl.CostEstimate(flops=0, bytes_accessed=int(micros * 3.69e6), transcendentals=0)


def any_space():
    return pl.BlockSpec(memory_space=pltpu.MemorySpace.HBM)


def split_kernel(cols, rows, x_ref, _, __, planes_ref, north_ref, south_ref, hold, P, sem, out_sem):
    count = HALO - 1
    loads = [pltpu.make_async_copy(x_ref.at[c], hold.at[c], sem.at[c]) for c in range(3)]
    for copy in loads:
        copy.start()
    outs = []
    for c in range(3):
        loads[c].wait()
        for r in range(rows):
            P[c, r, pl.ds(8, cols)] = hold[c, pl.ds(r, cols, stride=rows), :]
        mine = [
            (P.at[c, pl.ds(0, count)], north_ref.at[pl.ds(count * c, count)]),
            (P.at[c, pl.ds(rows - count, count)], south_ref.at[pl.ds(count * c, count)]),
            (P.at[c], planes_ref.at[c]),
        ]
        if c == 2:
            mine.append((P.at[c, pl.ds(count, 1)], north_ref.at[pl.ds(3 * count, 1)]))
            mine.append((P.at[c, pl.ds(rows - HALO, 1)], south_ref.at[pl.ds(3 * count, 1)]))
        for s, d in mine:
            outs.append(pltpu.make_async_copy(s, d, out_sem.at[len(outs)]))
            outs[-1].start()
    for copy in outs:
        copy.wait()


def split_planes(flat, after, cols, rows):
    lev = flat.shape[-1]
    wide = window(cols)
    edge = jax.ShapeDtypeStruct((3 * (HALO - 1) + 1, wide, lev), f32)
    planes = (3, rows, wide, lev)
    return pl.pallas_call(
        functools.partial(split_kernel, cols, rows),
        in_specs=[any_space()] * 3,
        out_specs=[any_space()] * 3,
        out_shape=[jax.ShapeDtypeStruct(planes, f32), edge, edge],
        scratch_shapes=[
            pltpu.VMEM(flat.shape, f32),
            pltpu.VMEM(planes, f32),
            pltpu.SemaphoreType.DMA((3,)),
            pltpu.SemaphoreType.DMA((11,)),
        ],
        compiler_params=params(60),
    )(flat, *after)


def column_kernel(cols, rows, west_ref, east_ref, _, __, north_ref, south_ref, W, E, sem, out_sem):
    at = (8 + cols) // 8 * 8
    off = 8 + cols - at
    ends = ((north_ref, 0), (south_ref, 1))
    loads = [pltpu.make_async_copy(ref.at[:, pl.ds(at, 16)], E.at[k], sem.at[k]) for ref, k in ends]
    for copy in loads:
        copy.start()
    for k, (base, last) in enumerate(((0, HALO - 1), (rows - HALO + 1, rows - HALO))):
        planes = [(c, base + j) for c in range(3) for j in range(HALO - 1)] + [(2, last)]
        for n, (c, r) in enumerate(planes):
            W[k, n, pl.ds(8 - HALO, HALO)] = west_ref[c, pl.ds(r, HALO, stride=rows), :]
        loads[k].wait()
        for n, (c, r) in enumerate(planes):
            E[k, n, pl.ds(off, HALO)] = east_ref[c, pl.ds(r, HALO, stride=rows), :]
    outs = [pltpu.make_async_copy(E.at[k], ref.at[:, pl.ds(at, 16)], sem.at[k]) for ref, k in ends]
    outs += [pltpu.make_async_copy(W.at[k], ref.at[:, pl.ds(0, 8)], out_sem.at[k]) for ref, k in ends]
    for copy in outs:
        copy.start()
    for copy in outs:
        copy.wait()


def with_columns(west, east_, north, south, cols, rows):
    count, _, lev = north.shape
    return pl.pallas_call(
        functools.partial(column_kernel, cols, rows),
        in_specs=[vmem(), vmem(), any_space(), any_space()],
        out_specs=[any_space()] * 2,
        out_shape=[jax.ShapeDtypeStruct(north.shape, f32)] * 2,
        scratch_shapes=[
            pltpu.VMEM((2, count, 8, lev), f32),
            pltpu.VMEM((2, count, 16, lev), f32),
            pltpu.SemaphoreType.DMA((2,)),
            pltpu.SemaphoreType.DMA((2,)),
        ],
        input_output_aliases={2: 0, 3: 1},
        compiler_params=params(4),
    )(west, east_, north, south)


def east(W, r):
    cols = W.shape[1] - 16
    return W[r, pl.ds(9, cols)] - W[r, pl.ds(7, cols)]


def stage_steps(metric_ref, base, U, V, T, A, B, C, keep):
    mid = pl.ds(8, U.shape[1] - 16)

    def metric(i):
        return metric_ref[i + (HALO - base)]

    def advect(i, fields=None):
        mu = metric(i) * (0.5 * ADV) * U[i, mid]
        nv = (0.5 * ADV) * V[i, mid]
        for W, out in fields or ((U, A), (V, B), (T, C)):
            out[i, mid] = W[i, mid] - (mu * east(W, i) + nv * (W[i + 1, mid] - W[i - 1, mid]))

    def advect_theta(i):
        advect(i, ((T, C),))

    def wind_u(i):
        A[i, mid] = A[i, mid] - (metric(i) * (0.5 * SOUND)) * east(C, i)

    def wind_v(i):
        B[i, mid] = keep(i, B[i, mid] - (0.5 * SOUND) * (C[i + 1, mid] - C[i - 1, mid]))

    def theta(i):
        m = metric(i) * (0.5 * SOUND)
        C[i, mid] = keep(i, C[i, mid] - (m * east(A, i) + (0.5 * SOUND) * (B[i + 1, mid] - B[i - 1, mid])))

    return advect, advect_theta, wind_u, wind_v, theta


def sweep(fn, *spans):
    for lo, hi in spans:

        def step(i, carry):
            fn(i)
            return carry

        lax.fori_loop(lo, hi, step, 0, unroll=UNROLL)


def inner_kernel(
    cols, rows, metric_ref, planes_ref, west_ref, east_ref, off_ref, _, u_ref, v_ref, theta_ref, rim_ref, raw_ref, *scratch
):
    U, V, T, A, B, C, sem, out_sem = scratch
    own = slice(LEAD, LEAD + cols)
    wide = pl.ds(LEAD - 8, window(cols))
    loads = [pltpu.make_async_copy(planes_ref.at[c], W.at[:, wide], sem.at[c]) for c, W in enumerate((U, V, T))]
    for copy in loads:
        copy.start()
    outs = []
    for c, W in enumerate((U, V, T)):
        loads[c].wait()

        for r in range(rows):
            W[r, pl.ds(LEAD - HALO, HALO)] = west_ref[c, pl.ds(r, HALO, stride=rows), :]
            W[r, pl.ds(LEAD + cols, HALO)] = east_ref[c, pl.ds(r, HALO, stride=rows), :]
        for k, at in ((0, 0), (1, rows - 2)):
            outs.append((W.at[pl.ds(at, 2), wide], raw_ref.at[c, pl.ds(2 * k, 2)]))
    advect, _, wind_u, wind_v, theta = stage_steps(metric_ref, 0, U, V, T, A, B, C, lambda r, x: x)
    sweep(advect, (1, rows - 1))
    sweep(wind_u, (1, rows - 1))
    sweep(wind_v, (2, rows - 2))
    sweep(theta, (3, rows - 3))
    sweep(wind_u, (3, rows - 3))
    sweep(wind_v, (4, rows - 4))
    sweep(theta, (5, rows - 5))
    for c, W in enumerate((A, B, C)):
        for k, at in ((0, 1), (1, rows - 6)):
            outs.append((W.at[pl.ds(at, 5), wide], rim_ref.at[c, pl.ds(5 * k, 5)]))
    outs = [pltpu.make_async_copy(a, b, out_sem.at[i]) for i, (a, b) in enumerate(outs)]
    for copy in outs:
        copy.start()
    pad = padded(cols)
    for d in range(GROUP):
        u_ref[d, pl.ds(0, cols)] = A[INNER[d], own]
        u_ref[d, pl.ds(cols, PACK)] = off_ref[PACK * d : PACK * (d + 1)]
        v_ref[d, pl.ds(0, cols)] = B[INNER[d], own]
        theta_ref[d, pl.ds(0, cols)] = C[INNER[d], own]
    for copy in outs:
        copy.wait()


def inner_rows(metric, planes, west, east_, offsets, after, cols, rows):
    lev = planes.shape[-1]
    pad = padded(cols)
    wide = window(cols)
    shapes = [(GROUP, pad, lev)] * 3 + [(3, 10, wide, lev), (3, 4, wide, lev)]
    return pl.pallas_call(
        functools.partial(inner_kernel, cols, rows),
        in_specs=[smem(), any_space(), vmem(), vmem(), vmem(), any_space()],
        out_specs=[vmem()] * 3 + [any_space()] * 2,
        out_shape=[jax.ShapeDtypeStruct(s, f32) for s in shapes],
        scratch_shapes=[pltpu.VMEM((rows, LEAD + wide, lev), f32)] * 6
        + [pltpu.SemaphoreType.DMA((3,)), pltpu.SemaphoreType.DMA((12,))],
        compiler_params=params(60),
        cost_estimate=cost(9),
    )(metric, planes, west, east_, offsets, after)


def edge_kernel(cols, rows, near_pole, ids_ref, *refs):
    @pl.when((ids_ref[3] != 0) if near_pole else (ids_ref[3] == 0))
    def _():
        edge_steps(cols, rows, near_pole, ids_ref, *refs)


def edge_steps(
    cols, rows, near_pole, ids_ref, metric_ref, raw_ref, rim_ref, hn_ref, hs_ref, u_ref, v_ref, theta_ref, _, out_ref, *scratch
):
    U, V, T, A, B, C, sem, move_sem, *more = scratch
    own = slice(LEAD, LEAD + cols)
    wide = pl.ds(LEAD - 8, window(cols))
    pad = padded(cols)
    count = HALO - 1
    loads = []
    for c, W in enumerate((U, V, T)):
        loads.append((hn_ref.at[pl.ds(count * c, count)], W.at[pl.ds(1, count), wide]))
        loads.append((hs_ref.at[pl.ds(count * c, count)], W.at[pl.ds(HALO + rows, count), wide]))
        loads.append((raw_ref.at[c, pl.ds(0, 2)], W.at[pl.ds(HALO, 2), wide]))
        loads.append((raw_ref.at[c, pl.ds(2, 2)], W.at[pl.ds(HALO + rows - 2, 2), wide]))
    loads.append((hn_ref.at[pl.ds(3 * count, 1)], T.at[pl.ds(0, 1), wide]))
    loads.append((hs_ref.at[pl.ds(3 * count, 1)], T.at[pl.ds(2 * HALO + rows - 1, 1), wide]))
    for c, W in enumerate((A, B, C)):
        loads.append((rim_ref.at[c, pl.ds(0, 5)], W.at[pl.ds(HALO + 1, 5), wide]))
        loads.append((rim_ref.at[c, pl.ds(5, 5)], W.at[pl.ds(HALO + rows - 6, 5), wide]))
    loads = [pltpu.make_async_copy(a, b, sem.at[i]) for i, (a, b) in enumerate(loads)]
    for copy in loads:
        copy.start()
    for copy in loads[:14]:
        copy.wait()
    has_north = jnp.where(ids_ref[1] > 0, 1.0, 0.0)
    has_south = jnp.where(ids_ref[2] > 0, 1.0, 0.0)

    def keep(i, x):
        return x * jnp.where(i >= HALO + rows, has_south, jnp.where(i < HALO, has_north, 1.0))

    advect, advect_theta, wind_u, wind_v, theta = stage_steps(metric_ref, HALO, U, V, T, A, B, C, keep)

    def ends(fn, lo, hi):
        sweep(fn, (HALO + lo, HALO + hi), (HALO + rows - hi, HALO + rows - lo))

    ends(advect, -3, 1)
    ends(advect_theta, -4, -3)
    for copy in loads[14:]:
        copy.wait()
    ends(wind_u, -2, 1)
    ends(wind_v, -3, 2)
    ends(theta, -2, 3)
    ends(wind_u, 0, 3)
    ends(wind_v, -1, 4)
    ends(theta, 0, 5)

    if near_pole:
        inside = pltpu.make_async_copy(
            theta_ref.at[pl.ds(1, GROUP - 2)], out_ref.at[pl.ds(1, GROUP - 2), pl.ds(3 * pad, pad)], move_sem.at[0]
        )
        inside.start()
        for d in range(GROUP):
            for c, W in enumerate((A, B, C)):
                out_ref[d, pl.ds(c * pad, cols)] = W[EDGE[d] + HALO, own]
        for d in (0, GROUP - 1):
            out_ref[d, pl.ds(3 * pad, cols)] = C[INNER[d] + HALO, own]
        inside.wait()
    else:
        hold, moved, out_sem = more
        inside = [
            pltpu.make_async_copy(ref, moved.at[:, pl.ds(c * pad, pad)], move_sem.at[c])
            for c, ref in enumerate((u_ref, v_ref, theta_ref))
        ]
        for copy in inside:
            copy.start()
        for copy in inside:
            copy.wait()
        outs = [pltpu.make_async_copy(hold.at[c], out_ref.at[c], out_sem.at[c]) for c in range(3)]
        for c, W in enumerate((A, B, C)):
            for d in range(GROUP):
                hold[c, pl.ds(EDGE[d], cols, stride=rows), :] = W[EDGE[d] + HALO, own]
                if c == 2 and d in (0, GROUP - 1):
                    value = C[INNER[d] + HALO, own]
                else:
                    value = moved[d, pl.ds(c * pad, cols)]
                hold[c, pl.ds(INNER[d], cols, stride=rows), :] = value
            outs[c].start()
        for out in outs:
            out.wait()


def edge_rows(near_pole, ids, metric, raw, rim, hn, hs, inner, after, cols, rows):
    lev = raw.shape[-1]
    pad = padded(cols)
    whole = (3, cols * rows, lev)
    scratch = [pltpu.VMEM((rows + 2 * HALO, LEAD + window(cols), lev), f32)] * 6
    scratch += [pltpu.SemaphoreType.DMA((20,)), pltpu.SemaphoreType.DMA((3,))]
    if not near_pole:
        scratch += [pltpu.VMEM(whole, f32), pltpu.VMEM((GROUP, 3 * pad, lev), f32), pltpu.SemaphoreType.DMA((3,))]
    return pl.pallas_call(
        functools.partial(edge_kernel, cols, rows, near_pole),
        in_specs=[smem(), smem()] + [any_space()] * 8,
        out_specs=vmem() if near_pole else any_space(),
        out_shape=jax.ShapeDtypeStruct((GROUP, 4 * pad, lev) if near_pole else whole, f32),
        scratch_shapes=scratch,
        compiler_params=params(57 if near_pole else 60),
    )(ids, metric, raw, rim, hn, hs, *inner, after)


def offset_tables(length):
    half = length // 2
    pad = -(-half // 256) * 256
    n = np.arange(2 * pad) - pad
    tables = []
    for first in (0, 1):
        wave = np.arange(first, half + 1, 2)
        weight = np.where((wave == 0) | (wave == half), 1.0, 2.0) / length
        angle = (wave[:, None] * n[None, :]) % length * (2.0 * np.pi / length)
        tables.append((wave, (np.cos(angle) * weight[:, None]).astype(np.float32)))
    return tables


def offset_values(limits, length):
    values = []
    for wave, table in offset_tables(length):
        w = jnp.asarray(wave, f32)
        lim = limits[:, None]
        factor = jnp.where(w[None, :] <= lim, 1.0, (lim / jnp.maximum(w, 1.0)[None, :]) ** 2)
        values.append(jnp.dot(factor, jnp.asarray(table), precision=lax.Precision.HIGHEST, preferred_element_type=f32))
    return jnp.stack(values, axis=1)[:, :, None, :]


def skew(p, store):
    width = p.shape[-1]
    line = lax.broadcasted_iota(jnp.int32, (8, width), 0)
    x = jnp.broadcast_to(p, (8, width))
    for bit in range(3):
        x = jnp.where((line & (1 << bit)) != 0, pltpu.roll(x, 1 << bit, 1), x)
    for pair in range(8):
        two = [pltpu.roll(x, 8 * g, 1)[:, 128:] if g else x[:, 128:] for g in (2 * pair, 2 * pair + 1)]
        y = jnp.concatenate(two, axis=0)
        hi = y.astype(bf16)
        store(16 * pair, hi, (y - hi.astype(f32)).astype(bf16))


def unpack_kernel(length, x_ref, _, hi_ref, lo_ref):
    cols = length // GROUP
    lines = [x_ref[d, cols + j : cols + j + 1] for d in range(GROUP) for j in range(PACK)]
    half = len(lines) // 2
    for e in range(2):

        def store(at, hi, lo, e=e):
            hi_ref[0, e, at : at + 16] = hi
            lo_ref[0, e, at : at + 16] = lo

        skew(jnp.concatenate(lines[e * half : (e + 1) * half], axis=1), store)


def unpacked(x, length, after):
    width = GROUP * PACK * x.shape[-1] // 2
    out = jax.ShapeDtypeStruct((1, 2, 128, width - 128), bf16)
    return pl.pallas_call(
        functools.partial(unpack_kernel, length),
        in_specs=[vmem(), any_space()],
        out_specs=[vmem()] * 2,
        out_shape=[out, out],
        compiler_params=params(16),
    )(x, after)


def skew_kernel(p_ref, _, hi_ref, lo_ref):
    rows, parts, _, width = p_ref.shape
    for r in range(rows):
        for e in range(parts):

            def store(at, hi, lo, r=r, e=e):
                hi_ref[r, e, at : at + 16] = hi
                lo_ref[r, e, at : at + 16] = lo

            skew(p_ref[r, e], store)


def skewed(values, after):
    rows, parts, _, width = values.shape
    out = jax.ShapeDtypeStruct((rows, parts, 128, width - 128), bf16)
    return pl.pallas_call(
        skew_kernel,
        in_specs=[vmem(), any_space()],
        out_specs=[vmem()] * 2,
        out_shape=[out, out],
        compiler_params=params(16),
    )(values, after)


def filter_kernel(groups, cols, hi_ref, lo_ref, x_ref, _, y_ref, S, D, Y, Z):
    quarter = GROUP // 2
    size = S.shape[0]
    lev = x_ref.shape[-1]
    pad = padded(cols)
    units = [u for _, members in groups for u in members]
    S[quarter * cols :] = jnp.zeros((size - quarter * cols, S.shape[1]), f32)
    D[quarter * cols :] = jnp.zeros((size - quarter * cols, S.shape[1]), f32)
    for b in range(quarter):
        at = slice(b * cols, (b + 1) * cols)
        for i, u in enumerate(units):
            lanes = slice(i * lev, (i + 1) * lev)
            one = x_ref[b, pl.ds(u * pad, cols)]
            two = x_ref[b + quarter, pl.ds(u * pad, cols)]
            S[at, lanes] = one + two
            D[at, lanes] = one - two
    tall = size // 128
    first = 0
    for row, members in groups:
        lanes = slice(first * lev, (first + len(members)) * lev)
        first += len(members)

        def matrix(ref, e, row=row):
            starts = [(tall - 1 - b) * 128 for b in range(tall)]
            return jnp.concatenate([ref[row, e, :, st : st + size] for st in starts], axis=0)

        for e, (src, dst) in enumerate(((S, Y), (D, Z))):
            x = src[:, lanes]
            xh = x.astype(bf16)
            xl = (x - xh.astype(f32)).astype(bf16)
            mh = matrix(hi_ref, e)
            ml = matrix(lo_ref, e)
            if len(members) == 1:
                both = jnp.dot(mh, jnp.concatenate([xh, xl], axis=1), preferred_element_type=f32)
                small = jnp.dot(ml, xh, preferred_element_type=f32)
                dst[:, lanes] = both[:, :lev] + (both[:, lev:] + small)
            else:
                left = jnp.concatenate([mh, mh, ml], axis=1)
                right = jnp.concatenate([xh, xl, xh], axis=0)
                dst[:, lanes] = jnp.dot(left, right, preferred_element_type=f32)
    for b in range(quarter):
        at = slice(b * cols, (b + 1) * cols)
        for i, u in enumerate(units):
            lanes = slice(i * lev, (i + 1) * lev)
            y = Y[at, lanes]
            z = Z[at, lanes]
            y_ref[b, pl.ds(u * pad, cols)] = y + z
            y_ref[b + quarter, pl.ds(u * pad, cols)] = y - z


def filtered(groups, hi, lo, whole, after, cols):
    _, tall, lev = whole.shape
    count = sum(len(members) for _, members in groups)
    work = pltpu.VMEM((hi.shape[-1] - 128 * 5, count * lev), f32)
    return pl.pallas_call(
        functools.partial(filter_kernel, groups, cols),
        in_specs=[vmem()] * 3 + [any_space()],
        out_specs=vmem(),
        out_shape=jax.ShapeDtypeStruct(whole.shape, f32),
        scratch_shapes=[work] * 4,
        compiler_params=params(28),
    )(hi, lo, whole, after)


def join_kernel(cols, rows, ids_ref, y_ref, u_ref, v_ref, _, out_ref, held, moved, result, sem, out_sem):
    @pl.when(ids_ref[3] != 0)
    def _():
        pad = padded(cols)
        copies = [pltpu.make_async_copy(y_ref.at[:, pl.ds(u * pad, pad)], held.at[u], sem.at[u]) for u in range(4)]
        copies += [pltpu.make_async_copy(ref, moved.at[u], sem.at[4 + u]) for u, ref in enumerate((u_ref, v_ref))]
        outs = [pltpu.make_async_copy(result.at[c], out_ref.at[c], out_sem.at[c]) for c in range(3)]
        for copy in copies:
            copy.start()
        for c, inner, wait in ((0, moved.at[0], 4), (1, moved.at[1], 5), (2, held.at[3], 3)):
            copies[c].wait()
            copies[wait].wait()
            for d in range(GROUP):
                result[c, pl.ds(EDGE[d], cols, stride=rows), :] = held[c, d, 0:cols]
                result[c, pl.ds(INNER[d], cols, stride=rows), :] = inner[d, 0:cols]
            outs[c].start()
        for c in range(3):
            outs[c].wait()


def joined(ids, whole, moved_u, moved_v, other, cols, rows):
    lev = whole.shape[-1]
    pad = padded(cols)
    return pl.pallas_call(
        functools.partial(join_kernel, cols, rows),
        in_specs=[smem()] + [any_space()] * 4,
        out_specs=any_space(),
        out_shape=jax.ShapeDtypeStruct(other.shape, f32),
        scratch_shapes=[
            pltpu.VMEM((4, GROUP, pad, lev), f32),
            pltpu.VMEM((2, GROUP, pad, lev), f32),
            pltpu.VMEM(other.shape, f32),
            pltpu.SemaphoreType.DMA((6,)),
            pltpu.SemaphoreType.DMA((3,)),
        ],
        input_output_aliases={4: 0},
        compiler_params=params(16),
    )(ids, whole, moved_u, moved_v, other)


def tie_kernel(x_ref, _, out_ref):
    pass


def tied(x, y):
    return pl.pallas_call(
        tie_kernel,
        in_specs=[any_space()] * 2,
        out_specs=any_space(),
        out_shape=jax.ShapeDtypeStruct(x.shape, x.dtype),
        input_output_aliases={0: 0},
        compiler_params=params(1),
    )(x, y)


def hollow_kernel(out_ref):
    pass


def hollow(x):
    return pl.pallas_call(
        hollow_kernel,
        out_specs=any_space(),
        out_shape=jax.ShapeDtypeStruct(x.shape, x.dtype),
        compiler_params=params(1),
    )()


def swapped(x):
    return lax.all_to_all(x, "lon", split_axis=0, concat_axis=0, tiled=True)


def body(state, cutoffs):
    lat_count = lax.axis_size("lat")
    lon_count = lax.axis_size("lon")
    _, cols, rows, lev = state.shape
    total_lat = rows * lat_count
    total_lon = cols * lon_count
    band = lax.axis_index("lat")
    me = lax.axis_index("lon")
    quarter = lat_count // 4
    polar = (band < quarter) | (band >= lat_count - quarter)
    ids = jnp.stack([me, band, lat_count - 1 - band, polar.astype(jnp.int32)]).astype(jnp.int32)

    up = [(i, i + 1) for i in range(lat_count - 1)]
    down = [(j, i) for i, j in up]
    right = [(i, (i + 1) % lon_count) for i in range(lon_count)]
    left = [(j, i) for i, j in right]

    flat = state.reshape(3, cols * rows, lev)
    last = state[:, cols - HALO :].reshape(3, HALO * rows, lev)
    first = state[:, :HALO].reshape(3, HALO * rows, lev)
    east_ = lax.ppermute(first, "lon", left)
    west = lax.ppermute(last, "lon", right)
    outward = [(b, b + quarter) for b in range(quarter)]
    outward += [(b, b - quarter) for b in range(lat_count - quarter, lat_count)]
    inward = [(j, i) for i, j in outward]
    near = band * rows - HALO + jnp.arange(rows + 2 * HALO, dtype=jnp.int32)
    latitude = (-90.0 + (near.astype(f32) + 0.5) * (180.0 / total_lat)) * (jnp.pi / 180.0)
    metric = 1.0 / jnp.maximum(jnp.cos(latitude), 1.0 / CAP)

    planes, own_north, own_south = split_planes(flat, (last, first), cols, rows)
    send_north, send_south = with_columns(west, east_, own_north, own_south, cols, rows)
    wanted = jnp.stack([edge_row(me), inner_row(me)])
    chosen = wanted[:, None] == jnp.arange(rows, dtype=jnp.int32)[None, :]
    picked = jnp.sum(jnp.where(chosen, cutoffs.astype(f32)[None, :], 0.0), axis=1)
    picked = tied(picked, send_north)
    offsets = offset_values(picked, total_lon)
    token = jnp.zeros((8, lev), f32)
    packed = offsets[1].reshape(GROUP * PACK, lev)
    hi, lo = skewed(offsets, token)
    halo_north = lax.ppermute(send_south, "lat", up)
    halo_south = lax.ppermute(send_north, "lat", down)

    u, v, theta, rim, raw = inner_rows(metric, planes, west, east_, packed, send_north, cols, rows)
    moved_u = lax.ppermute(u, "lat", outward)
    moved_v = lax.ppermute(v, "lat", outward)
    def edges(near_pole, after):
        inner = (u, v, theta)
        return edge_rows(near_pole, ids, metric, raw, rim, halo_north, halo_south, inner, after, cols, rows)

    def elsewhere(x, first, after):
        hi, lo = unpacked(first, total_lon, after)
        return swapped(filtered(((0, (0,)),), hi, lo, swapped(x), after, cols))

    def idle(x, *_):
        return hollow(x)

    def near_pole(x, after):
        return swapped(filtered(((0, (0, 1)), (0, (2,)), (1, (3,))), hi, lo, x, after, cols))

    def same(x, *_):
        return x

    def first_half(after):
        return swapped(edges(True, after))

    blank = jax.ShapeDtypeStruct((GROUP, 4 * padded(cols), lev), f32)
    whole = lax.cond(polar, first_half, lambda _: hollow(blank), lo)
    back_u = lax.cond(polar, idle, elsewhere, moved_u, moved_u, tied(token, whole))
    moved_back_u = lax.ppermute(back_u, "lat", inward)
    back_v = lax.cond(polar, idle, elsewhere, moved_v, moved_u, tied(token, whole))
    moved_back_v = lax.ppermute(back_v, "lat", inward)
    other = lax.cond(polar, lambda _: hollow(flat), lambda after: edges(False, after), tied(token, back_v))
    pieces = lax.cond(polar, near_pole, same, whole, tied(token, back_v))
    return joined(ids, pieces, moved_back_u, moved_back_v, other, cols, rows).reshape(3, cols, rows, lev)


def solution(mesh):
    placed = (P(None, "lon", "lat", None), P("lat"))
    return jax.shard_map(
        body, mesh=mesh, in_specs=placed, out_specs=P(None, "lon", "lat", None), check_vma=False
    )
```
